128 devices in a mesh: blk: 128 (over x, y, z, core).
Axes of the slice: x: 4, y: 4, z: 4, core: 2. Of those that a mesh axis runs over, the one named last changes fastest.
Arguments:
- tokens: bfloat16 [16384, 768], P('blk'), may hold values from -6 to 6
- store_keys: bfloat16 [8192, 768], P('blk'), may hold values from -9 to 9
- store_values: bfloat16 [8192, 768], P('blk'), may hold values from -6 to 6
- retrieved: int32 [16384, 1024], P('blk'), may hold values from 0 to 8191, as said below
- seq_lengths: int32 [128], P('blk'), may hold values from 64 to 128, as said below
- w_query: bfloat16 [768, 768], replicated, may hold values from -0.21875 to 0.21875
- w_key: bfloat16 [768, 768], replicated, may hold values from -0.4375 to 0.4375
- w_value: bfloat16 [768, 768], replicated, may hold values from -0.21875 to 0.21875
- w_out: bfloat16 [768, 768], replicated, may hold values from -0.875 to 0.875
- c_query: bfloat16 [768, 768], replicated, may hold values from -0.21875 to 0.21875
- c_out: bfloat16 [768, 768], replicated, may hold values from -0.875 to 0.875
- ffn_in: bfloat16 [768, 3072], replicated, may hold values from -0.21875 to 0.21875
- ffn_bias: float32 [3072], replicated, may hold values from -3 to 3
- ffn_out: bfloat16 [3072, 768], replicated, may hold values from -0.109375 to 0.109375
- gain_self: float32 [768], replicated, may hold values from 0.5 to 1.5
- shift_self: float32 [768], replicated, may hold values from -2 to 2
- gain_cross: float32 [768], replicated, may hold values from 0.5 to 1.5
- shift_cross: float32 [768], replicated, may hold values from -2 to 2
- gain_ffn: float32 [768], replicated, may hold values from 0.5 to 1.5
- shift_ffn: float32 [768], replicated, may hold values from -2 to 2
- cotangent: float32 [16384, 768], P('blk'), may hold values from -24 to 24
Outputs:
- block_output: float32 [16384, 768], P('blk')
- d_tokens: float32 [16384, 768], P('blk')
- d_store_keys: float32 [8192, 768], P('blk')
- d_store_values: float32 [8192, 768], P('blk')
- d_w_query: float32 [768, 768], P('blk')
- d_w_key: float32 [768, 768], P('blk')
- d_w_value: float32 [768, 768], P('blk')
- d_w_out: float32 [768, 768], P('blk')
- d_c_query: float32 [768, 768], P('blk')
- d_c_out: float32 [768, 768], P('blk')
- d_ffn_in: float32 [768, 3072], P('blk')
- d_ffn_bias: float32 [3072], P('blk')
- d_ffn_out: float32 [3072, 768], P('blk')
- d_gain_self: float32 [768], P('blk')
- d_shift_self: float32 [768], P('blk')
- d_gain_cross: float32 [768], P('blk')
- d_shift_cross: float32 [768], P('blk')
- d_gain_ffn: float32 [768], P('blk')
- d_shift_ffn: float32 [768], P('blk')
The draws below stay inside these ranges and needn't reach their ends.
Inputs may be any that keep to these rules, and one draw needn't show every extreme that they name: `retrieved`: each row names 1024 different datastore rows. `seq_lengths`: positions from a sequence's length on are padding; some sequence has none.
All inputs are finite; a program needn't handle non-finite values.
Results may differ from the reference program's by a relative error of at most 0.035.
Values may be sent and summed in bfloat16 or wider, within the bound.
No kernel may reach another device: no remote copies, remote signals or barrier semaphores. Data moves between devices by JAX's collectives and lax.ppermute only.
A program may use at most 320 MiB of HBM per device.

```python
import jax
import jax.numpy as jnp
from jax import lax

D = 768
HEADS = 12
HEAD_DIM = 64
FF = 3072
TOK_DEV = 128
K_TOP = 1024
SEQS = 128
TOKENS = 16384
STORE = 8192


def draw_retrieved(key, part):
    key = jax.random.fold_in(key, 11)

    def one_row(row_key):
        noise = jax.random.randint(row_key, (STORE,), 0, 2 ** 30 // STORE)
        ranked = noise * STORE + jnp.arange(STORE, dtype=jnp.int32)
        return lax.top_k(ranked, K_TOP)[1].astype(jnp.int32)
    row_keys = jax.random.split(key, TOKENS)
    row_keys = row_keys.reshape((SEQS, TOK_DEV) + row_keys.shape[1:])
    picked = lax.map(jax.vmap(one_row), row_keys)
    return picked.reshape(TOKENS, K_TOP).astype(jnp.int32)


def draw_seq_lengths(key, part):
    key = jax.random.fold_in(key, 5)
    first_key, second_key = jax.random.split(key)
    lengths = jax.random.randint(first_key, (SEQS,), TOK_DEV // 2, TOK_DEV + 1)
    chosen = jax.random.randint(second_key, (), 0, SEQS)
    lengths = jnp.where(jnp.arange(SEQS) == chosen, TOK_DEV, lengths)
    return lengths.astype(jnp.int32)


def spiked(array, key, source, target, shards_of, factor):
    def block_of(dim):
        return (jnp.arange(array.shape[dim]) // (array.shape[dim] // shards_of)).reshape((-1,) + (1,) * (array.ndim - 1 - dim))

    near = jax.random.permutation(key, shards_of)[block_of(target)]
    other_side = (block_of(target) + shards_of // 2) % shards_of
    return jnp.where((block_of(source) == near) | (block_of(source) == other_side), factor * array, array)


def block_levels(own_key, dims, cuts, smallest, high):
    loudness = 1.0
    for dim, shards_of in cuts:
        heights = jax.random.uniform(jax.random.fold_in(jax.random.fold_in(own_key, 6), dim), (shards_of,), jnp.float32, smallest / len(cuts), high / len(cuts))
        loudness = loudness * jnp.repeat(jnp.exp(heights), dims[dim] // shards_of).reshape((-1,) + (1,) * (len(dims) - 1 - dim))
    return loudness


def normal_values(stream_key, shape, spread, bound, pieces=(), held_as=jnp.bfloat16):
    result = spread * jax.random.normal(stream_key, shape, jnp.float32)
    if pieces:
        result = result * block_levels(stream_key, shape, pieces, -0.22, 0.18)
    return jnp.clip(result, -bound, bound).astype(held_as)


def noise_with(own_key, shape, width, limit, pieces, heavy, held_as=jnp.bfloat16):
    array = width * jax.random.normal(own_key, shape, jnp.float32)
    if pieces:
        array = array * block_levels(own_key, shape, pieces, -0.22, 0.18)
    return jnp.clip(spiked(array, jax.random.fold_in(own_key, 3), *heavy), -limit, limit).astype(held_as)


def setup_inputs(seed: int = 0) -> dict:
    keys = jax.random.split(jax.random.key(seed), 22)
    return {
        "tokens": normal_values(keys[0], (TOKENS, D), 1.0, 6.0, ((0, 128),)),
        "store_keys": normal_values(keys[1], (STORE, D), 1.5, 9.0, ((0, 128),)),
        "store_values": normal_values(keys[2], (STORE, D), 1.0, 6.0, ((0, 128),)),
        "retrieved": draw_retrieved(jax.random.fold_in(keys[21], 71), 0),
        "seq_lengths": draw_seq_lengths(jax.random.fold_in(keys[21], 71), 0),
        "w_query": normal_values(keys[5], (D, D), D ** -0.5, 0.21875),
        "w_key": normal_values(keys[6], (D, D), (D // 4) ** -0.5, 0.4375),
        "w_value": normal_values(keys[7], (D, D), D ** -0.5, 0.21875),
        "w_out": normal_values(keys[8], (D, D), (D // 16) ** -0.5, 0.875),
        "c_query": normal_values(keys[9], (D, D), D ** -0.5, 0.21875),
        "c_out": normal_values(keys[10], (D, D), (D // 16) ** -0.5, 0.875),
        "ffn_in": normal_values(keys[11], (D, FF), D ** -0.5, 0.21875),
        "ffn_bias": normal_values(keys[12], (FF,), 0.5, 3.0, (), jnp.float32),
        "ffn_out": normal_values(keys[13], (FF, D), FF ** -0.5, 0.109375),
        "gain_self": jnp.clip(1.0 + 0.1 * jax.random.normal(keys[14], (D,), jnp.float32), 0.5, 1.5),
        "shift_self": normal_values(keys[15], (D,), 0.3, 2.0, (), jnp.float32),
        "gain_cross": jnp.clip(1.0 + 0.1 * jax.random.normal(keys[16], (D,), jnp.float32), 0.5, 1.5),
        "shift_cross": normal_values(keys[17], (D,), 0.3, 2.0, (), jnp.float32),
        "gain_ffn": jnp.clip(1.0 + 0.1 * jax.random.normal(keys[18], (D,), jnp.float32), 0.5, 1.5),
        "shift_ffn": normal_values(keys[19], (D,), 0.3, 2.0, (), jnp.float32),
        "cotangent": noise_with(keys[20], (TOKENS, D), 1.0, 24.0, ((0, 128),), (0, 1, 128, 5.5), jnp.float32),
    }


HIGHEST = lax.Precision.HIGHEST

@jax.custom_vjp
def low(v):
    return lax.optimization_barrier(v.astype(jnp.bfloat16)).astype(jnp.float32)

@jax.custom_vjp
def low_back(v):
    return v

def low_keep(v):
    return (low(v), None)

def low_pass(kept, grad):
    return (grad,)

def back_keep(v):
    return (v, None)

def back_low(kept, grad):
    return (low(grad),)
low.defvjp(low_keep, low_pass)
low_back.defvjp(back_keep, back_low)

def rounded_both(value):
    return low(low_back(value))

def product(operand_one, operand_two):
    return jnp.dot(operand_one, operand_two, precision=HIGHEST)

def layer_norm(summed, norm_gain, norm_shift):
    average = lax.optimization_barrier(jnp.mean(summed, -1, keepdims=True))
    centred = summed - average
    variance = lax.optimization_barrier(jnp.mean(centred * centred, -1, keepdims=True))
    return centred * lax.rsqrt(variance + 1e-05) * norm_gain + norm_shift

def reference(tokens, store_keys, store_values, retrieved, seq_lengths, w_query, w_key, w_value, w_out, c_query, c_out, ffn_in, ffn_bias, ffn_out, gain_self, shift_self, gain_cross, shift_cross, gain_ffn, shift_ffn, cotangent):
    scaling = HEAD_DIM ** (-0.5)
    block_rows = 16
    position = jnp.arange(TOK_DEV)
    causal = position[None, :] <= position[:, None]
    unpadded = position[None, :] < seq_lengths[:, None]
    allowed = causal[None, None, :, :] & unpadded[:, None, None, :]
    index_blocks = retrieved.reshape(TOKENS // block_rows, block_rows, K_TOP)

    def forward(hidden, keys_all, values_all, wq, wk, wv, wo, cq, co, first, bias, second, gone, sone, gtwo, stwo, gthree, sthree):
        queries = rounded_both(product(hidden, wq)).reshape(SEQS, TOK_DEV, HEADS, HEAD_DIM)
        keys_self = rounded_both(product(hidden, wk)).reshape(SEQS, TOK_DEV, HEADS, HEAD_DIM)
        values_self = rounded_both(product(hidden, wv)).reshape(SEQS, TOK_DEV, HEADS, HEAD_DIM)
        raw_scores = jnp.einsum('sqhd,skhd->shqk', queries, keys_self, precision=HIGHEST)
        scores = jnp.where(allowed, low_back(raw_scores) * scaling, -1e+30)
        weights_self = jax.nn.softmax(scores, axis=-1)
        attended = jnp.einsum('shqk,skhd->sqhd', low(weights_self), values_self, precision=HIGHEST)
        attended = rounded_both(attended.reshape(TOKENS, D))
        hidden_one = layer_norm(hidden + low_back(product(attended, wo)), gone, sone)
        cross_queries = rounded_both(product(low(hidden_one), cq)).reshape(TOKENS // block_rows, block_rows, HEADS, HEAD_DIM)

        def cross_block(operands):
            query_block, index_block = operands
            key_rows = keys_all[index_block].reshape(block_rows, K_TOP, HEADS, HEAD_DIM)
            value_rows = values_all[index_block].reshape(block_rows, K_TOP, HEADS, HEAD_DIM)
            raw_block = jnp.einsum('bhd,bkhd->bhk', query_block, key_rows, precision=HIGHEST)
            weights_block = jax.nn.softmax(low_back(raw_block) * scaling, axis=-1)
            return jnp.einsum('bhk,bkhd->bhd', low(weights_block), value_rows, precision=HIGHEST)
        cross_full = lax.map(jax.checkpoint(cross_block), (cross_queries, index_blocks))
        cross_out = rounded_both(cross_full.reshape(TOKENS, D))
        hidden_two = layer_norm(hidden_one + low_back(product(cross_out, co)), gtwo, stwo)
        pre_act = low_back(product(low(hidden_two), first) + bias)
        activated = low(jax.nn.gelu(pre_act, approximate=False))
        return layer_norm(hidden_two + low_back(product(activated, second)), gthree, sthree)
    floats = (tokens.astype(jnp.float32), store_keys.astype(jnp.float32), store_values.astype(jnp.float32), w_query.astype(jnp.float32), w_key.astype(jnp.float32), w_value.astype(jnp.float32), w_out.astype(jnp.float32), c_query.astype(jnp.float32), c_out.astype(jnp.float32), ffn_in.astype(jnp.float32), ffn_bias.astype(jnp.float32), ffn_out.astype(jnp.float32), gain_self, shift_self, gain_cross, shift_cross, gain_ffn, shift_ffn)
    block_output, pullback = jax.vjp(forward, *floats)
    gradients = pullback(cotangent.astype(jnp.float32))
    return (block_output, gradients[0], gradients[1], gradients[2], gradients[3], gradients[4], gradients[5], gradients[6], gradients[7], gradients[8], gradients[9], gradients[10], gradients[11], gradients[12], gradients[13], gradients[14], gradients[15], gradients[16], gradients[17])
```

```python
import functools
import math

import jax
import jax.numpy as jnp
from jax import lax
from jax.experimental import pallas as pl
from jax.experimental.pallas import tpu as pltpu
from jax.sharding import Mesh, PartitionSpec as P

F32 = jnp.float32
BF = jnp.bfloat16
LOWEST = -1e30
LOG2E = math.log2(math.e)
SCALE = 64 ** (-0.5)
CHIP = ("x", "y", "z")
ALL = ("x", "y", "z", "c")
ORDERS = (("x", "y", "z"), ("y", "z", "x"), ("z", "x", "y"))


def low(v):
    return v.astype(BF)


def nn(a, b):
    return jnp.dot(a, b, preferred_element_type=F32)


def nt(a, b):
    return lax.dot_general(a, b, (((1,), (1,)), ((), ())), preferred_element_type=F32)


def tn(a, b):
    return lax.dot_general(a, b, (((0,), (0,)), ((), ())), preferred_element_type=F32)


def mask_body(ret_ref, out_ref, m_ref):
    hi_io=lax.broadcasted_iota(jnp.int32,(64,1024),0)
    lo_io=lax.broadcasted_iota(jnp.int32,(128,1024),0)
    def group(g,_):
        idx=ret_ref[pl.ds(pl.multiple_of(g*8,8),8),:]
        hi=idx>>7; lo=idx&127
        for j in range(8):
            hh=jnp.where(hi_io==hi[j:j+1,:],1.0,0.0).astype(BF)
            ll=jnp.where(lo_io==lo[j:j+1,:],1.0,0.0).astype(BF)
            m_ref[g*8+j]=nt(hh,ll)
        return 0
    lax.fori_loop(0,16,group,0)
    def flip(h,_):
        blk=m_ref[:,h,:]
        out_ref[h]=(blk.T-1.0)*(1e30)
        return 0
    lax.fori_loop(0,64,flip,0)

def make_mask(retrieved):
    return pl.pallas_call(mask_body,
        out_shape=jax.ShapeDtypeStruct((64,128,128),F32),
        in_specs=[pl.BlockSpec(memory_space=pltpu.VMEM)],
        out_specs=pl.BlockSpec(memory_space=pltpu.VMEM),
        scratch_shapes=[pltpu.VMEM((128,64,128),F32)],
        compiler_params=pltpu.CompilerParams(vmem_limit_bytes=48*2**20),
        name="mask")(retrieved)

def fwd_body(k_ref,v_ref,b0_ref,b1_ref,ct_ref,x_ref,l_ref,acc,ms,ls,*,sub):
    step=pl.program_id(1)
    @pl.when(step==0)
    def _():
        acc[...]=jnp.zeros_like(acc)
        ms[...]=jnp.full_like(ms,LOWEST)
        ls[...]=jnp.zeros_like(ls)
    nsub=k_ref.shape[0]//sub
    def one(i,_):
        sl=pl.ds(i*sub,sub)
        r=sub*128
        kk=k_ref[sl].reshape(r,128)
        vt=v_ref[sl].reshape(r,128).T
        bias=jnp.concatenate([b0_ref[sl].reshape(r,128),b1_ref[sl].reshape(r,128)],1)
        for h in range(2):
            t=nn(kk,ct_ref[0,h])*(LOG2E*0.125)+bias
            m_old=ms[h]
            m_new=jnp.maximum(m_old,jnp.max(t,0,keepdims=True))
            p=jnp.exp2(t-m_new)
            a=jnp.exp2(m_old-m_new)
            ls[h]=ls[h]*a+jnp.sum(p,0,keepdims=True)
            ms[h]=m_new
            acc[h]=acc[h]*a+nn(vt[h*64:(h+1)*64],p.astype(BF))
        return 0
    lax.fori_loop(0,nsub,one,0)
    @pl.when(step==pl.num_programs(1)-1)
    def _():
        xs=[]
        for h in range(2):
            xs.append(acc[h]/ls[h])
            l_ref[0,h]=ms[h]+jnp.log2(ls[h])
        x_ref[...]=jnp.concatenate(xs,0).T

def cross_fwd(kv,b0,b1,ct,blk=16,sub=4):
    nb=64//blk
    return pl.pallas_call(functools.partial(fwd_body,sub=sub),
        grid=(3,nb),
        in_specs=[pl.BlockSpec((blk,128,128),lambda p,i:(i,0,p)),
                  pl.BlockSpec((blk,128,128),lambda p,i:(i,0,p+3)),
                  pl.BlockSpec((blk,128,128),lambda p,i:(i,0,0)),
                  pl.BlockSpec((blk,128,128),lambda p,i:(i,0,0)),
                  pl.BlockSpec((1,2,128,256),lambda p,i:(p,0,0,0))],
        out_specs=[pl.BlockSpec((256,128),lambda p,i:(0,p)),
                   pl.BlockSpec((1,2,1,256),lambda p,i:(p,0,0,0))],
        out_shape=[jax.ShapeDtypeStruct((256,384),F32),jax.ShapeDtypeStruct((3,2,1,256),F32)],
        scratch_shapes=[pltpu.VMEM((2,64,256),F32),pltpu.VMEM((2,1,256),F32),pltpu.VMEM((2,1,256),F32)],
        compiler_params=pltpu.CompilerParams(vmem_limit_bytes=56*2**20),
        name="cross_fwd")(kv,kv,b0,b1,ct)

def bwd_body(me_ref,k_ref,v_ref,b0_ref,b1_ref,ct_ref,dxt_ref,c_ref,dx_ref,l_ref,dl_ref,o0,o1,o2,o3,dc_ref,*,part):
    d=pl.program_id(0)
    @pl.when(d==0)
    def _():
        dc_ref[...]=jnp.zeros_like(dc_ref)
    def pick(ref,i):
        if part==0: blk=ref[0,i]
        elif part==1: blk=ref[:,0,i]
        else: blk=ref[i,:,0]
        return blk.reshape(512,128)
    outs=(o0,o1,o2,o3)
    for i in range(4):
        kk=pick(k_ref,i); vv=pick(v_ref,i)
        kt=kk.T
        bias=jnp.concatenate([pick(b0_ref,i),pick(b1_ref,i)],1)
        dk=0.;dv=0.
        for h in range(2):
            p=jnp.exp2(nn(kk,ct_ref[h])*(LOG2E*0.125)+bias-l_ref[h])
            dp=nn(vv,dxt_ref[h])-dl_ref[h]
            ds=(p*dp).astype(BF)
            pb=p.astype(BF)
            dv=dv+nn(pb,dx_ref[h])
            dk=dk+nn(ds,c_ref[h])
            dc_ref[h*64:(h+1)*64]+=nn(kt[h*64:(h+1)*64],ds)
        res=jnp.concatenate([dk,dv],1).astype(BF).reshape(4,128,256)
        for j in range(4):
            @pl.when(d==j)
            def _(j=j):
                outs[j][i*4:(i+1)*4]=res

def cross_bwd(me,kv,b0,b1,ct,dxt,c,dx,l,dl,part):
    if part==0:
        shp=(1,4,4); im=lambda d,me:((d+me[0])%4,0,0)
    elif part==1:
        shp=(4,1,4); im=lambda d,me:(0,(d+me[0])%4,0)
    else:
        shp=(4,4,1); im=lambda d,me:(0,0,(d+me[0])%4)
    full=lambda s: pl.BlockSpec(s,lambda d,me:(0,)*len(s))
    sp=lambda col: pl.BlockSpec(shp+(128,128),lambda d,me:im(d,me)+(0,col))
    return pl.pallas_call(functools.partial(bwd_body,part=part),
        grid_spec=pltpu.PrefetchScalarGridSpec(num_scalar_prefetch=1,grid=(4,),
        in_specs=[sp(part),sp(part+3),sp(0),sp(0),full((2,128,256)),full((2,128,256)),full((2,256,128)),full((2,256,128)),full((2,1,256)),full((2,1,256))],
        out_specs=[full((16,128,256))]*4+[full((128,256))]),
        out_shape=[jax.ShapeDtypeStruct((16,128,256),BF)]*4+[jax.ShapeDtypeStruct((128,256),F32)],
        compiler_params=pltpu.CompilerParams(vmem_limit_bytes=56*2**20),
        name="cross_bwd%d"%part)(me,kv,kv,b0,b1,ct,dxt,c,dx,l,dl)


def layer_norm(summed, gain, shift):
    average = jnp.mean(summed, -1, keepdims=True)
    centred = summed - average
    spread = lax.rsqrt(jnp.mean(centred * centred, -1, keepdims=True) + 1e-05)
    normed = centred * spread
    return normed * gain + shift, normed, spread


def norm_back(upstream, normed, spread, gain):
    scaled = upstream * gain
    grad = spread * (
        scaled
        - jnp.mean(scaled, -1, keepdims=True)
        - normed * jnp.mean(scaled * normed, -1, keepdims=True)
    )
    here = slice(0, 256)
    return grad, jnp.sum((upstream * normed)[here], 0), jnp.sum(upstream[here], 0)


def swap(v):
    return lax.ppermute(v, "c", [(0, 1), (1, 0)])


def shift_by(v, axis, d):
    return lax.ppermute(v, axis, [(i, (i + d) % 4) for i in range(4)])


def both(v):
    return jnp.concatenate([v, swap(v)], 0)


def pair_sum(partial):
    other = swap(partial)
    half = partial.shape[0] // 2
    return partial + jnp.concatenate([other[half:], other[:half]], 0)


def scatter_axis(v, dim, axis):
    n = v.shape[dim] // 4
    me = lax.axis_index(axis)
    total = lax.dynamic_slice_in_dim(v, me * n, n, dim).astype(F32)
    for d in (1, 2, 3):
        piece = lax.dynamic_slice_in_dim(v, lax.rem(me + d, 4) * n, n, dim)
        total = total + shift_by(piece, axis, d).astype(F32)
    return total


def scatter_all(v, dim, order):
    for number, axis in enumerate(order):
        v = scatter_axis(v, dim, axis)
        if number < 2:
            v = low(v)
    return v


def head_pad(a):
    six = a.T.reshape(3, 2, 64, 256)
    zero = jnp.zeros_like(six[:, 0])
    return jnp.stack(
        [jnp.concatenate([six[:, 0], zero], 1), jnp.concatenate([zero, six[:, 1]], 1)], 1
    )


def place_matrix(order):
    row = jnp.arange(768)
    chip, unit = row // 12, row % 12
    at = {"x": chip // 16, "y": chip // 4 % 4, "z": chip % 4}
    turned = (at[order[0]] * 4 + at[order[1]]) * 4 + at[order[2]]
    return low((unit * 64 + turned)[:, None] == jnp.arange(768)[None, :])


def shards(
    tokens, store_keys, store_values, retrieved, seq_lengths,
    w_query, w_key, w_value, w_out, c_query, c_out, ffn_in, ffn_bias, ffn_out,
    gain_self, shift_self, gain_cross, shift_cross, gain_ffn, shift_ffn, cotangent,
):
    core = lax.axis_index("c")
    first = core == 0

    def columns(w):
        n = w.shape[1] // 2
        return lax.dynamic_slice_in_dim(w, core * n, n, 1)

    def other_columns(w):
        n = w.shape[1] // 2
        return lax.dynamic_slice_in_dim(w, (1 - core) * n, n, 1)

    def rows(w):
        n = w.shape[0] // 2
        return lax.dynamic_slice_in_dim(w, core * n, n, 0)

    def in_order(mine, other, dim):
        return jnp.where(
            first,
            jnp.concatenate([mine, other], dim),
            jnp.concatenate([other, mine], dim),
        )

    kv_mine = jnp.concatenate([columns(store_keys), columns(store_values)], 1)
    kv_other = swap(jnp.concatenate([other_columns(store_keys), other_columns(store_values)], 1))
    kv_chip = in_order(kv_mine, kv_other, 0)
    kv = lax.all_gather(kv_chip, CHIP, axis=0, tiled=True)

    bias_own = make_mask(retrieved)
    bias_other = swap(bias_own)

    tok = both(tokens)
    cot = both(cotangent)
    lengths = both(seq_lengths)

    def heads(a):
        return a.reshape(2, 128, 6, 64).transpose(0, 2, 1, 3)

    def joined(a):
        return a.transpose(0, 2, 1, 3).reshape(256, 384)

    wq, wk, wv, wo = columns(w_query), columns(w_key), columns(w_value), rows(w_out)
    cq, co = columns(c_query), rows(c_out)
    fi, fb, fo = columns(ffn_in), lax.dynamic_slice_in_dim(ffn_bias, core * 1536, 1536, 0), rows(ffn_out)
    q = heads(low(nn(tok, wq)))
    k = heads(low(nn(tok, wk)))
    v = heads(low(nn(tok, wv)))
    place = jnp.arange(128)
    allowed = (place[None, :] <= place[:, None])[None] & (
        place[None, None, :] < lengths[:, None, None]
    )
    raw = jnp.einsum("bhqd,bhkd->bhqk", q, k, preferred_element_type=F32)
    scores = jnp.where(allowed[:, None], raw * SCALE, LOWEST)
    shifted = jnp.exp(scores - jnp.max(scores, -1, keepdims=True))
    probs = shifted / jnp.sum(shifted, -1, keepdims=True)
    low_probs = low(probs)
    o_full = jnp.einsum("bhqk,bhkd->bhqd", low_probs, v, preferred_element_type=F32)
    o = joined(low(o_full))
    h1, n1, r1 = layer_norm(tok.astype(F32) + pair_sum(nn(o, wo)), gain_self, shift_self)
    low1 = low(h1)
    c = low(nn(low1, cq))
    c_pad = head_pad(c)

    x_full, lse = cross_fwd(kv.reshape(64, 128, 768), bias_own, bias_other, c_pad)
    x = low(x_full)
    h2, n2, r2 = layer_norm(h1 + pair_sum(nn(x, co)), gain_cross, shift_cross)
    low2 = low(h2)
    pre = nn(low2, fi) + fb
    act, gelu_back = jax.vjp(functools.partial(jax.nn.gelu, approximate=False), pre)
    g = low(act)
    out, n3, r3 = layer_norm(h2 + pair_sum(nn(g, fo)), gain_ffn, shift_ffn)

    e3, d_gain_ffn, d_shift_ffn = norm_back(cot, n3, r3, gain_ffn)
    f = low(e3)
    du = low(gelu_back(nt(f, fo))[0])
    d_bias = jnp.sum(du.astype(F32), 0)
    e2, d_gain_cross, d_shift_cross = norm_back(e3 + pair_sum(nt(du, fi)), n2, r2, gain_cross)
    y = low(e2)

    swapped_g = swap(g)
    g_all = in_order(g, jnp.concatenate([swapped_g[128:], swapped_g[:128]], 0), 1)
    swapped_x = swap(x)
    x_all = in_order(x, jnp.concatenate([swapped_x[128:], swapped_x[:128]], 0), 1)
    swapped_o = swap(o)
    o_all = in_order(o, jnp.concatenate([swapped_o[128:], swapped_o[:128]], 0), 1)
    places = [place_matrix(order) for order in ORDERS]

    def placed(a, p):
        return low(nn(a, places[p]))

    def weight_grad(a, b, p):
        return low(tn(placed(a, p), b)).reshape(12, 64, b.shape[1])

    gr_in = scatter_all(weight_grad(low2, du, 0), 1, ORDERS[0])
    gr_out = low(tn(g_all, columns(f))).reshape(4, 4, 4, 48, 384)
    for number, (dim, axis) in enumerate(((1, "y"), (2, "z"), (0, "x"))):
        gr_out = scatter_axis(gr_out, dim, axis)
        gr_out = low(gr_out) if number < 2 else gr_out
    gr_co = scatter_all(weight_grad(x_all, columns(y), 2), 1, ORDERS[2])

    dx = low(nt(y, co))
    delta = SCALE * jnp.sum((dx.astype(F32) * x_full).reshape(256, 6, 64), -1).T.reshape(3, 2, 1, 256)
    dx_pad = head_pad(dx)
    c_rows = c_pad.transpose(0, 1, 3, 2)
    dx_rows = dx_pad.transpose(0, 1, 3, 2)
    dx_scaled = dx_pad * jnp.asarray(SCALE, BF)
    kv6 = kv.reshape(4, 4, 4, 128, 768)
    own6 = bias_own.reshape(4, 4, 4, 128, 128)
    other6 = bias_other.reshape(4, 4, 4, 128, 128)
    dcs, store_grads = [], []
    for p, order in enumerate(ORDERS):
        me = lax.axis_index(order[0]).reshape(1)
        pieces = cross_bwd(
            me, kv6, own6, other6, c_pad[p], dx_scaled[p], c_rows[p], dx_rows[p], lse[p], delta[p], p
        )
        dcs.append(pieces[4])
        total = pieces[0].astype(F32)
        for d in (1, 2, 3):
            total = total + shift_by(pieces[d], order[0], d).astype(F32)
        total = low(total).reshape(4, 4, 128, 256)
        total = low(scatter_axis(total, 0, order[1])[0])
        store_grads.append(scatter_axis(total, 0, order[2])[0])
    dc = low(jnp.concatenate(dcs, 0).T)

    e1, d_gain_self, d_shift_self = norm_back(e2 + pair_sum(nt(dc, cq)), n1, r1, gain_self)
    z = low(e1)

    do = heads(low(nt(z, wo)))
    eps = jnp.sum(do.astype(F32) * o_full, -1, keepdims=True)
    dp = jnp.einsum("bhqd,bhkd->bhqk", do, v, preferred_element_type=F32)
    ds = low(probs * (dp - eps) * SCALE)
    dq = joined(low(jnp.einsum("bhqk,bhkd->bhqd", ds, k, preferred_element_type=F32)))
    dk = joined(low(jnp.einsum("bhqk,bhqd->bhkd", ds, q, preferred_element_type=F32)))
    dv = joined(low(jnp.einsum("bhqk,bhqd->bhkd", low_probs, do, preferred_element_type=F32)))
    d_tok = pair_sum(nt(dq, wq) + nt(dk, wk) + nt(dv, wv))[:128] + e1[:128]

    vectors = jnp.where(
        first,
        jnp.stack([d_gain_self, d_gain_cross, d_gain_ffn]),
        jnp.stack([d_shift_self, d_shift_cross, d_shift_ffn]),
    )
    zero_bias = jnp.zeros_like(d_bias)
    bias_all = in_order(d_bias, zero_bias, 0).reshape(64, 12, 4)
    small = jnp.concatenate([vectors.reshape(3, 64, 12).transpose(1, 2, 0), bias_all], 2)
    small = jnp.pad(small.transpose(1, 0, 2), ((0, 0), (0, 0), (0, 121)))
    small = small.reshape(12, 4, 4, 4, 128).transpose(0, 3, 1, 2, 4).reshape(12, 64, 128)

    late = []
    late.append(jnp.concatenate([weight_grad(tok, dq, 0), weight_grad(low1, dc, 0)], 2))
    late.append(jnp.concatenate([weight_grad(tok, dk, 1), weight_grad(o_all, columns(z), 1)], 2))
    late.append(jnp.concatenate([weight_grad(tok, dv, 2), low(small)], 2))
    late = [scatter_all(a, 1, order) for a, order in zip(late, ORDERS)]

    def finish(a, n):
        mine, theirs = a.reshape(2, n, a.shape[-1]), None
        theirs = swap(lax.dynamic_index_in_dim(mine, 1 - core, 0, False))
        return lax.dynamic_index_in_dim(mine, core, 0, False), theirs

    wide = jnp.concatenate([a[:, 0] for a in late] + [gr_co[:, 0], gr_in[:, 0]], 1)
    mine, theirs = finish(wide, 6)

    def take(start, size):
        return in_order(mine[:, start : start + size], theirs[:, start : start + size], 1)

    d_wq, d_cq, d_wk, d_wo, d_wv = (take(s, 384) for s in (0, 384, 768, 1152, 1536))
    d_co, d_fi = take(2048, 384), take(2432, 1536)
    s_mine, s_theirs = mine[:, 1920:2048], theirs[:, 1920:2048]
    gains = jnp.where(first, s_mine[:, :3], s_theirs[:, :3])
    shifts = jnp.where(first, s_theirs[:, :3], s_mine[:, :3])
    d_fb = (s_mine[:, 3:7] + s_theirs[:, 3:7]).reshape(24)
    out_mine, out_theirs = finish(gr_out[0, 0, 0] if gr_out.ndim == 5 else gr_out, 24)
    d_fo = in_order(out_mine, out_theirs, 1)
    store = jnp.concatenate(store_grads, 1).reshape(128, 3, 2, 128)
    store = store.transpose(0, 2, 1, 3).reshape(128, 768)
    st_mine, st_theirs = finish(store, 64)
    d_keys = in_order(st_mine[:, :384], st_theirs[:, :384], 1)
    d_values = in_order(st_mine[:, 384:], st_theirs[:, 384:], 1)
    return (
        out[:128], d_tok, d_keys, d_values, d_wq, d_wk, d_wv, d_wo, d_cq, d_co, d_fi, d_fb, d_fo,
        gains[:, 0], shifts[:, 0], gains[:, 1], shifts[:, 1], gains[:, 2], shifts[:, 2],
    )


def solution(mesh):
    grid = Mesh(mesh.devices.reshape(4, 4, 4, 2), ALL)
    split, line, whole = P(ALL, None), P(ALL), P()
    return jax.shard_map(
        shards,
        mesh=grid,
        in_specs=(split,) * 4 + (line,) + (whole,) * 15 + (split,),
        out_specs=(split,) * 11 + (line,) + (split,) + (line,) * 6,
        check_vma=False,
    )
```

```python
import functools
import math

import jax
import jax.numpy as jnp
from jax import lax
from jax.experimental import pallas as pl
from jax.experimental.pallas import tpu as pltpu
from jax.sharding import Mesh, PartitionSpec as P

F32 = jnp.float32
BF = jnp.bfloat16
LOWEST = -1e30
LOG2E = math.log2(math.e)
SCALE = 64 ** (-0.5)
CHIP = ("x", "y", "z")
ALL = ("x", "y", "z", "c")
ORDERS = (("x", "y", "z"), ("y", "z", "x"), ("z", "x", "y"))


def low(v):
    return v.astype(BF)


def nn(a, b):
    return jnp.dot(a, b, preferred_element_type=F32)


def nt(a, b):
    return lax.dot_general(a, b, (((1,), (1,)), ((), ())), preferred_element_type=F32)


def tn(a, b):
    return lax.dot_general(a, b, (((0,), (0,)), ((), ())), preferred_element_type=F32)


def mask_body(ret_ref, out_ref, m_ref):
    hi_io = lax.broadcasted_iota(jnp.int32, (64, 1024), 0)
    lo_io = lax.broadcasted_iota(jnp.int32, (128, 1024), 0)

    def group(g, carry):
        idx = ret_ref[pl.ds(pl.multiple_of(g * 8, 8), 8), :]
        hi, lo = idx >> 7, idx & 127
        for j in range(8):
            hot_hi = jnp.where(hi_io == hi[j : j + 1, :], 1.0, 0.0).astype(BF)
            hot_lo = jnp.where(lo_io == lo[j : j + 1, :], 1.0, 0.0).astype(BF)
            m_ref[g * 8 + j] = nt(hot_hi, hot_lo)
        return carry

    lax.fori_loop(0, 16, group, 0)

    def flip(h, carry):
        out_ref[h] = (m_ref[:, h, :].T - 1.0) * 1e30
        return carry

    lax.fori_loop(0, 64, flip, 0)


VM = pl.BlockSpec(memory_space=pltpu.VMEM)
BIG = pltpu.CompilerParams(vmem_limit_bytes=56 * 2**20)


def cost(us):
    return pl.CostEstimate(flops=int(us * 1e9), bytes_accessed=int(us * 3e6), transcendentals=0)


def shaped(shape, dtype=F32):
    return jax.ShapeDtypeStruct(shape, dtype)


def make_mask(retrieved):
    return pl.pallas_call(
        mask_body,
        out_shape=shaped((64, 128, 128)),
        in_specs=[VM],
        out_specs=VM,
        scratch_shapes=[pltpu.VMEM((128, 64, 128), F32)],
        compiler_params=BIG,
        name="mask",
        cost_estimate=cost(25),
    )(retrieved)


def one_head(a, h, dim):
    at = lax.broadcasted_iota(jnp.int32, a.shape, dim)
    keep = (at < 64) if h == 0 else (at >= 64)
    return jnp.where(keep, a, jnp.zeros_like(a))


def fwd_body(k_ref, v_ref, b0_ref, b1_ref, c_ref, co_ref, x_ref, l_ref, part_ref, acc, ms, ls):
    pair, step = pl.program_id(0), pl.program_id(1)

    @pl.when(step == 0)
    def _():
        acc[...] = jnp.zeros_like(acc)
        ms[...] = jnp.full_like(ms, LOWEST)
        ls[...] = jnp.zeros_like(ls)

    ct = c_ref[...].astype(F32).T.astype(BF)
    subs = k_ref.shape[0] // 4
    kk = [k_ref[4 * i : 4 * i + 4].reshape(512, 128) for i in range(subs)]
    vt = [v_ref[4 * i : 4 * i + 4].reshape(512, 128).T for i in range(subs)]
    bias = [
        jnp.concatenate(
            [b0_ref[4 * i : 4 * i + 4].reshape(512, 128), b1_ref[4 * i : 4 * i + 4].reshape(512, 128)], 1
        )
        for i in range(subs)
    ]
    for h in range(2):
        ch = one_head(ct, h, 0)
        t = [nn(kk[i], ch) * (LOG2E * SCALE) + bias[i] for i in range(subs)]
        m_old = ms[h]
        m_new = m_old
        for i in range(subs):
            m_new = jnp.maximum(m_new, jnp.max(t[i], 0, keepdims=True))
        a = jnp.exp2(m_old - m_new)
        total, summed = ls[h] * a, acc[h] * a
        for i in range(subs):
            p = jnp.exp2(t[i] - m_new)
            total = total + jnp.sum(p, 0, keepdims=True)
            summed = summed + nn(vt[i][h * 64 : (h + 1) * 64], p.astype(BF))
        ls[h] = total
        ms[h] = m_new
        acc[h] = summed

    @pl.when(step == pl.num_programs(1) - 1)
    def _():
        xs = []
        for h in range(2):
            xs.append(acc[h] / ls[h])
            l_ref[0, h] = ms[h] + jnp.log2(ls[h])
        x = jnp.concatenate(xs, 0).T
        x_ref[...] = x
        add = nn(x.astype(BF), co_ref[...])

        @pl.when(pair == 0)
        def _():
            part_ref[...] = add

        @pl.when(pair > 0)
        def _():
            part_ref[...] += add


def cross_fwd(kv, b0, b1, c, co, blk=16):
    kv_at = lambda shift: pl.BlockSpec((blk, 128, 128), lambda p, i: (i, 0, p + shift))
    b_at = pl.BlockSpec((blk, 128, 128), lambda p, i: (i, 0, 0))
    return pl.pallas_call(
        fwd_body,
        grid=(3, 64 // blk),
        in_specs=[
            kv_at(0), kv_at(3), b_at, b_at,
            pl.BlockSpec((256, 128), lambda p, i: (0, p)),
            pl.BlockSpec((128, 768), lambda p, i: (p, 0)),
        ],
        out_specs=[
            pl.BlockSpec((256, 128), lambda p, i: (0, p)),
            pl.BlockSpec((1, 2, 1, 256), lambda p, i: (p, 0, 0, 0)),
            pl.BlockSpec((256, 768), lambda p, i: (0, 0)),
        ],
        out_shape=[shaped((256, 384)), shaped((3, 2, 1, 256)), shaped((256, 768))],
        scratch_shapes=[
            pltpu.VMEM((2, 64, 256), F32), pltpu.VMEM((2, 1, 256), F32), pltpu.VMEM((2, 1, 256), F32)
        ],
        compiler_params=BIG,
        name="cross_fwd",
        cost_estimate=cost(30),
    )(kv, kv, b0, b1, c, co)


def bwd_body(tab_ref, k_ref, v_ref, b0_ref, b1_ref, c_ref, dx_ref, x_ref, l_ref, init_ref, out, dc_ref, acc, *, part, last):
    g = pl.program_id(0)

    @pl.when(g == 0)
    def _():
        acc[...] = init_ref[...] if last else jnp.zeros_like(acc)

    def pick(ref, i):
        blk = ref[0, i] if part == 0 else ref[:, 0, i] if part == 1 else ref[i, :, 0]
        return blk.reshape(512, 128)

    mid, far = (part + 1) % 3, (part + 2) % 3
    c, dx = c_ref[...], dx_ref[...]
    ct = c.astype(F32).T.astype(BF)
    dxt = dx.astype(F32).T
    prod = dxt * x_ref[...].T * SCALE
    dxt = (dxt * SCALE).astype(BF)
    delta = [jnp.sum(prod[h * 64 : (h + 1) * 64], 0, keepdims=True) for h in range(2)]
    cth = [one_head(ct, h, 0) for h in range(2)]
    dxth = [one_head(dxt, h, 0) for h in range(2)]
    ch = [one_head(c, h, 1) for h in range(2)]
    dxh = [one_head(dx, h, 1) for h in range(2)]
    for i in range(4):
        kk, vv = pick(k_ref, i), pick(v_ref, i)
        kt = kk.T
        bias = jnp.concatenate([pick(b0_ref, i), pick(b1_ref, i)], 1)
        dk, dv = 0.0, 0.0
        for h in range(2):
            p = jnp.exp2(nn(kk, cth[h]) * (LOG2E * SCALE) + bias - l_ref[0, h])
            ds = (p * (nn(vv, dxth[h]) - delta[h])).astype(BF)
            dv = dv + nn(p.astype(BF), dxh[h])
            dk = dk + nn(ds, ch[h])
            acc[h * 64 : (h + 1) * 64] += nn(kt[h * 64 : (h + 1) * 64], ds)
        dk = dk.astype(BF).reshape(4, 128, 128)
        dv = dv.astype(BF).reshape(4, 128, 128)
        for k in range(4):
            at = tab_ref[12 + mid * 4 + i] * 4 + tab_ref[12 + far * 4 + k]
            out[0, at, 0:128] = dk[k]
            out[0, at, 128:256] = dv[k]

    @pl.when(g == 1)
    def _():
        dc_ref[...] = acc[...].T.astype(BF) if last else acc[...]


def cross_bwd(tab, kv, b0, b1, c, dx, x, lse, part, init):
    last = init is not None
    shape = ((1, 4, 4), (4, 1, 4), (4, 4, 1))[part]

    def at(g, tab):
        block = [0, 0, 0]
        block[part] = tab[part * 4 + g + (0 if last else 2)]
        return tuple(block)

    def spot(column):
        return pl.BlockSpec(shape + (128, 128), lambda g, tab: at(g, tab) + (0, column))

    whole = lambda s: pl.BlockSpec(s, lambda g, tab: (0,) * len(s))
    heads = pl.BlockSpec((256, 128), lambda g, tab: (0, part))
    dc = shaped((256, 128), BF) if last else shaped((128, 256))
    return pl.pallas_call(
        functools.partial(bwd_body, part=part, last=last),
        grid_spec=pltpu.PrefetchScalarGridSpec(
            num_scalar_prefetch=1,
            grid=(2,),
            in_specs=[
                spot(part), spot(part + 3), spot(0), spot(0), heads, heads, heads,
                pl.BlockSpec((1, 2, 1, 256), lambda g, tab: (part, 0, 0, 0)), whole((128, 256)),
            ],
            out_specs=[pl.BlockSpec((1, 16, 256, 128), lambda g, tab: (g, 0, 0, 0)), whole(dc.shape)],
            scratch_shapes=[pltpu.VMEM((128, 256), F32)],
        ),
        out_shape=[shaped((2, 16, 256, 128), BF), dc],
        compiler_params=BIG,
        name="cross_bwd",
        cost_estimate=cost(10),
    )(tab, kv, kv, b0, b1, c, dx, x, lse, init if last else jnp.zeros((128, 256), F32))


def norm_parts(summed, gain, shift):
    average = jnp.mean(summed, -1, keepdims=True)
    centred = summed - average
    spread = lax.rsqrt(jnp.mean(centred * centred, -1, keepdims=True) + 1e-05)
    normed = centred * spread
    return normed * gain + shift, normed, spread


def norm_grad(upstream, normed, spread, gain):
    scaled = upstream * gain
    grad = spread * (
        scaled
        - jnp.mean(scaled, -1, keepdims=True)
        - normed * jnp.mean(scaled * normed, -1, keepdims=True)
    )
    return grad, jnp.sum(upstream * normed, 0, keepdims=True), jnp.sum(upstream, 0, keepdims=True)


def crossed(mine_ref, theirs_ref):
    return jnp.concatenate(
        [mine_ref[0:128] + theirs_ref[128:256], mine_ref[128:256] + theirs_ref[0:128]], 0
    )


def ffn_fwd_body(mine, theirs, h1, gain, shift, fi, fb, fo, h2_ref, n2_ref, r2_ref, low2_ref, g_ref, gp_ref, part_ref):
    j = pl.program_id(0)

    @pl.when(j == 0)
    def _():
        h2, n2, r2 = norm_parts(h1[...] + crossed(mine, theirs), gain[...], shift[...])
        h2_ref[...] = h2
        n2_ref[...] = n2
        r2_ref[...] = r2
        low2_ref[...] = h2.astype(BF)
        part_ref[...] = jnp.zeros_like(part_ref)

    u = nn(low2_ref[...], fi[...]) + fb[...]
    cdf = 0.5 * (1.0 + lax.erf(u * (2.0**-0.5)))
    g = (u * cdf).astype(BF)
    g_ref[...] = g
    gp_ref[...] = cdf + u * (jnp.exp(-0.5 * u * u) * ((2.0 * math.pi) ** -0.5))
    part_ref[...] += nn(g, fo[...])


def ffn_fwd(mine, theirs, h1, gain, shift, fi, fb, fo):
    n = 384
    whole = lambda s: pl.BlockSpec(s, lambda j: (0,) * len(s))
    big, row = whole((256, 768)), whole((1, 768))
    lanes = lambda rows: pl.BlockSpec((rows, n), lambda j: (0, j))
    return pl.pallas_call(
        ffn_fwd_body,
        grid=(1536 // n,),
        in_specs=[big, big, big, row, row, lanes(768), lanes(1), pl.BlockSpec((n, 768), lambda j: (j, 0))],
        out_specs=[big, big, whole((256, 1)), big, lanes(256), lanes(256), big],
        out_shape=[
            shaped((256, 768)), shaped((256, 768)), shaped((256, 1)), shaped((256, 768), BF),
            shaped((256, 1536), BF), shaped((256, 1536)), shaped((256, 768)),
        ],
        compiler_params=BIG,
        name="ffn_fwd",
        cost_estimate=cost(7),
    )(mine, theirs, h1, gain, shift, fi, fb, fo)


def ffn_bwd_body(mine, theirs, h2, cot, gain, shift, fi, fo, gp, out_ref, e3_ref, f_ref, dg_ref, ds_ref, du_ref, db_ref, part_ref):
    j = pl.program_id(0)

    @pl.when(j == 0)
    def _():
        out, n3, r3 = norm_parts(h2[...] + crossed(mine, theirs), gain[...], shift[...])
        out_ref[...] = out[0:128]
        e3, dg_ref[...], ds_ref[...] = norm_grad(cot[...], n3, r3, gain[...])
        e3_ref[...] = e3
        f_ref[...] = e3.astype(BF)
        part_ref[...] = jnp.zeros_like(part_ref)

    du = (nt(f_ref[...], fo[...]) * gp[...]).astype(BF)
    du_ref[...] = du
    db_ref[...] = jnp.sum(du.astype(F32), 0, keepdims=True)
    part_ref[...] += nt(du, fi[...])


def ffn_bwd(mine, theirs, h2, cot, gain, shift, fi, fo, gp):
    n = 384
    whole = lambda s: pl.BlockSpec(s, lambda j: (0,) * len(s))
    big, row = whole((256, 768)), whole((1, 768))
    lanes = lambda rows: pl.BlockSpec((rows, n), lambda j: (0, j))
    return pl.pallas_call(
        ffn_bwd_body,
        grid=(1536 // n,),
        in_specs=[big, big, big, big, row, row, lanes(768), pl.BlockSpec((n, 768), lambda j: (j, 0)), lanes(256)],
        out_specs=[whole((128, 768)), big, big, row, row, lanes(256), lanes(1), big],
        out_shape=[
            shaped((128, 768)), shaped((256, 768)), shaped((256, 768), BF), shaped((1, 768)), shaped((1, 768)),
            shaped((256, 1536), BF), shaped((1, 1536)), shaped((256, 768)),
        ],
        compiler_params=BIG,
        name="ffn_bwd",
        cost_estimate=cost(7),
    )(mine, theirs, h2, cot, gain, shift, fi, fo, gp)


def cross_in_body(mine, theirs, e3, n2, r2, gain, co, e2_ref, y_ref, dg_ref, ds_ref, dx_ref):
    e2, dg_ref[...], ds_ref[...] = norm_grad(e3[...] + crossed(mine, theirs), n2[...], r2[...], gain[...])
    e2_ref[...] = e2
    y = e2.astype(BF)
    y_ref[...] = y
    dx_ref[...] = nt(y, co[...]).astype(BF)


def cross_in(mine, theirs, e3, n2, r2, gain, co):
    return pl.pallas_call(
        cross_in_body,
        in_specs=[VM] * 7,
        out_specs=[VM] * 5,
        out_shape=[shaped((256, 768)), shaped((256, 768), BF), shaped((1, 768)), shaped((1, 768)), shaped((256, 384), BF)],
        compiler_params=BIG,
        name="cross_in",
        cost_estimate=cost(4),
    )(mine, theirs, e3, n2, r2, gain, co)


def half_of(core_ref, a_ref):
    n = a_ref.shape[1] // 2
    return jnp.where(core_ref[0] == 0, a_ref[:, 0:n], a_ref[:, n:])


def joined_heads(core_ref, mine, theirs):
    other = jnp.concatenate([theirs[128:256], theirs[0:128]], 0)
    left = jnp.where(core_ref[0] == 0, mine[...], other)
    right = jnp.where(core_ref[0] == 0, other, mine[...])
    return jnp.concatenate([left, right], 1)


def early_body(core_ref, low2, du, x, x_theirs, y, g, g_theirs, f, pm, out):
    a = nn(low2[...], pm[...]).astype(BF).T
    for j in range(4):
        out[:, j * 16 : (j + 1) * 16, :] = (
            nn(a, du[:, j * 384 : (j + 1) * 384]).astype(BF).reshape(64, 16, 384)
        )
    a = nn(joined_heads(core_ref, x, x_theirs), pm[...]).astype(BF).T
    out[:, 64:80, :] = nn(a, half_of(core_ref, y)).astype(BF).reshape(64, 16, 384)
    g_all = joined_heads(core_ref, g, g_theirs)
    fh = half_of(core_ref, f)
    for j in range(4):
        block = nn(g_all[:, j * 768 : (j + 1) * 768].T, fh).astype(BF)
        out[j * 16 : (j + 1) * 16, 80:128, :] = block.reshape(16, 48, 384)


SM = pl.BlockSpec(memory_space=pltpu.SMEM)


def early_grads(*args):
    return pl.pallas_call(
        early_body,
        in_specs=[SM] + [VM] * 9,
        out_specs=VM,
        out_shape=shaped((64, 128, 384), BF),
        compiler_params=BIG,
        name="early_grads",
        cost_estimate=cost(8),
    )(*args)


def self_in_body(mine, theirs, e2, n1, r1, gain, wo, e1_ref, z_ref, dg_ref, ds_ref, do_ref):
    e1, dg_ref[...], ds_ref[...] = norm_grad(e2[...] + crossed(mine, theirs), n1[...], r1[...], gain[...])
    e1_ref[...] = e1[0:128]
    z = e1.astype(BF)
    z_ref[...] = z
    do_ref[...] = nt(z, wo[...]).astype(BF)


def self_bwd_body(mine, theirs, e2, n1, r1, gain, wo, q_ref, k_ref, v_ref, of_ref, len_ref, wq, wk, wv,
                  e1_ref, z_ref, dg_ref, ds_ref, dq_ref, dk_ref, dv_ref, part_ref, do_ref):
    self_in_body(mine, theirs, e2, n1, r1, gain, wo, e1_ref, z_ref, dg_ref, ds_ref, do_ref)
    at_q = lax.broadcasted_iota(jnp.int32, (128, 128), 0)
    at_k = lax.broadcasted_iota(jnp.int32, (128, 128), 1)
    for b in range(2):
        rows = slice(b * 128, (b + 1) * 128)
        allowed = (at_k <= at_q) & (at_k < len_ref[b])
        for pair in range(3):
            cols = slice(pair * 128, (pair + 1) * 128)
            q2, k2, v2, do2 = q_ref[rows, cols], k_ref[rows, cols], v_ref[rows, cols], do_ref[rows, cols]
            of2 = of_ref[rows, cols]
            prod = do2.astype(F32) * of2
            dq2, dk2, dv2 = 0.0, 0.0, 0.0
            for h in range(2):
                kh, vh, qh, doh = (one_head(a, h, 1) for a in (k2, v2, q2, do2))
                s = jnp.where(allowed, nt(q2, kh) * SCALE, LOWEST)
                p = jnp.exp(s - jnp.max(s, -1, keepdims=True))
                p = p / jnp.sum(p, -1, keepdims=True)
                eps = jnp.sum(one_head(prod, h, 1), -1, keepdims=True)
                ds = (p * (nt(do2, vh) - eps) * SCALE).astype(BF)
                dq2 = dq2 + nn(ds, kh)
                dk2 = dk2 + tn(ds, qh)
                dv2 = dv2 + tn(p.astype(BF), doh)
            dq_ref[rows, cols] = dq2.astype(BF)
            dk_ref[rows, cols] = dk2.astype(BF)
            dv_ref[rows, cols] = dv2.astype(BF)
    part_ref[...] = nt(dq_ref[...], wq[...]) + nt(dk_ref[...], wk[...]) + nt(dv_ref[...], wv[...])


def self_bwd(mine, theirs, e2, n1, r1, gain, wo, q, k, v, of, lengths, wq, wk, wv):
    half = shaped((256, 384), BF)
    return pl.pallas_call(
        self_bwd_body,
        in_specs=[VM] * 11 + [pl.BlockSpec(memory_space=pltpu.SMEM)] + [VM] * 3,
        out_specs=[VM] * 8,
        out_shape=[
            shaped((128, 768)), shaped((256, 768), BF), shaped((1, 768)), shaped((1, 768)),
            half, half, half, shaped((256, 768)),
        ],
        scratch_shapes=[pltpu.VMEM((256, 384), BF)],
        compiler_params=BIG,
        name="self_bwd",
        cost_estimate=cost(8),
    )(mine, theirs, e2, n1, r1, gain, wo, q, k, v, of, lengths, wq, wk, wv)


def self_fwd_body(tok, wq, wk, wv, wo, len_ref, q_ref, k_ref, v_ref, of_ref, o_ref, part_ref):
    t = tok[...]
    q_ref[...] = nn(t, wq[...]).astype(BF)
    k_ref[...] = nn(t, wk[...]).astype(BF)
    v_ref[...] = nn(t, wv[...]).astype(BF)
    at_q = lax.broadcasted_iota(jnp.int32, (128, 128), 0)
    at_k = lax.broadcasted_iota(jnp.int32, (128, 128), 1)
    for b in range(2):
        rows = slice(b * 128, (b + 1) * 128)
        allowed = (at_k <= at_q) & (at_k < len_ref[b])
        for pair in range(3):
            cols = slice(pair * 128, (pair + 1) * 128)
            q2, k2, v2 = q_ref[rows, cols], k_ref[rows, cols], v_ref[rows, cols]
            o2 = 0.0
            for h in range(2):
                s = jnp.where(allowed, nt(q2, one_head(k2, h, 1)) * SCALE, LOWEST)
                p = jnp.exp(s - jnp.max(s, -1, keepdims=True))
                p = p / jnp.sum(p, -1, keepdims=True)
                o2 = o2 + nn(p.astype(BF), one_head(v2, h, 1))
            of_ref[rows, cols] = o2
            o_ref[rows, cols] = o2.astype(BF)
    part_ref[...] = nn(o_ref[...], wo[...])


def self_fwd(tok, wq, wk, wv, wo, lengths):
    half = shaped((256, 384), BF)
    return pl.pallas_call(
        self_fwd_body,
        in_specs=[VM] * 5 + [pl.BlockSpec(memory_space=pltpu.SMEM)],
        out_specs=[VM] * 6,
        out_shape=[half, half, half, shaped((256, 384)), half, shaped((256, 768))],
        compiler_params=BIG,
        name="self_fwd",
        cost_estimate=cost(6),
    )(tok, wq, wk, wv, wo, lengths)


def self_out_body(mine, theirs, tok, gain, shift, cq, h1_ref, n1_ref, r1_ref, low1_ref, c_ref):
    h1, n1, r1 = norm_parts(tok[...].astype(F32) + crossed(mine, theirs), gain[...], shift[...])
    h1_ref[...] = h1
    n1_ref[...] = n1
    r1_ref[...] = r1
    low1 = h1.astype(BF)
    low1_ref[...] = low1
    c_ref[...] = nn(low1, cq[...]).astype(BF)


def self_out(mine, theirs, tok, gain, shift, cq):
    return pl.pallas_call(
        self_out_body,
        in_specs=[VM] * 6,
        out_specs=[VM] * 5,
        out_shape=[
            shaped((256, 768)), shaped((256, 768)), shaped((256, 1)), shaped((256, 768), BF), shaped((256, 384), BF)
        ],
        compiler_params=BIG,
        name="self_out",
        cost_estimate=cost(3),
    )(mine, theirs, tok, gain, shift, cq)


def late_body(core_ref, tok, low1, o, o_theirs, dq, dk, dv, dc, z, vec_a, vec_b, bias, pm0, pm1, pm2, sel_v, key_v, sel_b, key_b, *outs):
    def put(number, slot, a, pm_ref, b):
        full = nn(nn(a, pm_ref[...]).astype(BF).T, b)
        if number == 2:
            vec = jnp.where(core_ref[0] == 0, vec_a[...], vec_b[...]).astype(BF)
            extra = nn(sel_b[...] * bias[...].astype(BF), key_b[...])
            for v in range(3):
                extra = extra + nn(sel_v[...] * vec[v : v + 1, :], key_v[v])
            full = jnp.concatenate([full[:, 0:128] + extra, full[:, 128:]], 1)
        full = full.astype(BF)
        for lane in range(3):
            piece = full[:, lane * 128 : (lane + 1) * 128].reshape(4, 16, 16, 128)
            at = slice(slot * 48 + lane * 16, slot * 48 + lane * 16 + 16)
            for d in range(4):
                outs[number * 2 + d // 2][d % 2, :, at, :] = piece[d]

    put(0, 0, tok[...], pm0, dq[...])
    put(0, 1, low1[...], pm0, dc[...])
    put(1, 0, tok[...], pm1, dk[...])
    put(1, 1, joined_heads(core_ref, o, o_theirs), pm1, half_of(core_ref, z))
    put(2, 0, tok[...], pm2, dv[...])


def late_grads(*args):
    sizes = (96, 96, 48)
    return pl.pallas_call(
        late_body,
        in_specs=[SM] + [VM] * 19,
        out_specs=[VM] * 6,
        out_shape=[shaped((2, 16, sizes[n // 2], 128), BF) for n in range(6)],
        compiler_params=BIG,
        name="late_grads",
        cost_estimate=cost(10),
    )(*args)


def finish_body(core_ref, mine, theirs, e_mine, e_theirs, keys, values, wq, cq, wk, wo, wv, co, fi, fo, fb, g0, s0, g1, s1, g2, s2):
    first = core_ref[0] == 0

    def pick(size, half, base, lanes=slice(0, 128), early=False):
        a, b = (e_mine, e_theirs) if early else (mine, theirs)
        a, b = a[base : base + 2 * size, lanes], b[base : base + 2 * size, lanes]
        chosen = jnp.where(first, a, b) if half == 0 else jnp.where(first, b, a)
        return jnp.where(first, chosen[0:size], chosen[size:])

    bases = (0, 352, 704)
    for half in range(2):
        for p in range(3):
            lanes = slice(half * 384 + p * 128, half * 384 + (p + 1) * 128)
            keys[:, lanes] = pick(64, half, bases[p])
            values[:, lanes] = pick(64, half, bases[p] + 128)
        for lane in range(3):
            lanes = slice(half * 384 + lane * 128, half * 384 + (lane + 1) * 128)
            for ref, base in ((wq, 256), (cq, 304), (wk, 608), (wo, 656), (wv, 960)):
                ref[:, lanes] = pick(8, half, base + lane * 16)[0:6]
        wide = slice(0, 384)
        co[:, half * 384 : half * 384 + 384] = pick(8, half, 64, wide, True)[0:6]
        fo[:, half * 384 : half * 384 + 384] = pick(24, half, 80, wide, True)
        for j in range(4):
            fi[:, half * 1536 + j * 384 : half * 1536 + (j + 1) * 384] = pick(8, half, j * 16, wide, True)[0:6]
    small = [pick(8, half, 960) for half in range(2)]
    for half, refs in enumerate(((g0, g1, g2), (s0, s1, s2))):
        for v, ref in enumerate(refs):
            ref[...] = small[half][6:7, v * 6 : v * 6 + 6]
    fb[...] = small[0][7:8, 0:24] + small[1][7:8, 0:24]


def finish(core, mine, theirs, e_mine, e_theirs):
    w, row = shaped((6, 768)), shaped((1, 6))
    return pl.pallas_call(
        finish_body,
        in_specs=[pl.BlockSpec(memory_space=pltpu.SMEM)] + [VM] * 4,
        out_specs=[VM] * 17,
        out_shape=[
            shaped((64, 768)), shaped((64, 768)), w, w, w, w, w, w, shaped((6, 3072)), shaped((24, 768)),
            shaped((1, 24)), row, row, row, row, row, row,
        ],
        compiler_params=BIG,
        name="finish",
        cost_estimate=cost(2),
    )(core, mine, theirs, e_mine, e_theirs)


def swap(v):
    return lax.ppermute(v, "c", [(0, 1), (1, 0)])


def partner(v, axis, sign):
    pairs = []
    for i in range(4):
        for c in range(2):
            step = sign if (i + c) % 2 == 0 else -sign
            pairs.append((i * 2 + c, (i + step) % 4 * 2 + c))
    return lax.ppermute(v, (axis, "c"), pairs)


def both(v):
    return jnp.concatenate([v, swap(v)], 0)


def after(v, *earlier):
    return lax.optimization_barrier((v, earlier))[0]


def first_swap(send, axis, *earlier):
    return partner(after(send, *earlier), axis, 1)


def second_swap(keep, got, axis, *earlier):
    pass_on = low(keep[1].astype(F32) + got[1].astype(F32))
    return [keep[0], got[0], partner(after(pass_on, *earlier), axis, -1)]


def total(groups, rows):
    parts = [sum(a[rows].astype(F32) for a in arrays) for arrays in groups]
    return jnp.concatenate(parts, 1) if len(parts) > 1 else parts[0]


def next_axis(groups, axis):
    n = groups[0][0].shape[0] // 2
    send = low(total(groups, slice(n, 2 * n)))
    keep = total(groups, slice(0, n))
    send, keep = (a.reshape((2, n // 2) + a.shape[1:]) for a in (send, keep))
    return second_swap(keep, first_swap(send, axis), axis)


def slot_tables(me, core):
    step = jnp.where((me + core) % 2 == 0, 1, -1)
    at = jnp.stack([me, me - step, me + step, me + 2], 1) % 4
    away = (jnp.arange(4)[None] - me[:, None]) % 4
    slot = slot_of(away, step[:, None])
    return at, slot, step


def slot_of(away, step):
    near = jnp.where((away == 1) == (step > 0), 2, 1)
    return jnp.where(away == 0, 0, jnp.where(away == 2, 3, near))


def place_matrices(me, step):
    feature = jnp.arange(768)
    chip, rest = feature // 12, feature % 12
    slot = rest // 6 * 8 + rest % 6
    spots = jnp.stack([chip // 16, chip // 4 % 4, chip % 4])
    rel = slot_of((spots - me[:, None]) % 4, step[:, None])
    columns = jnp.arange(1024)
    natural = low((chip * 16 + slot)[:, None] == columns[None])
    turned = []
    for p in range(3):
        order = (rel[p] * 4 + rel[(p + 1) % 3]) * 4 + rel[(p + 2) % 3]
        turned.append(low((order * 16 + slot)[:, None] == columns[None]))
    order2 = (rel[2] * 4 + rel[0]) * 4 + rel[1]
    sel_v = low((order2 * 16 + rest // 6 * 8 + 6)[None] == columns[:, None])
    lane = jnp.arange(128)
    key_v = low(jnp.stack([(feature % 6 + 6 * v)[:, None] == lane[None] for v in range(3)]))
    return natural, turned, sel_v, key_v


def bias_matrices(me, step, core):
    feature = core * 1536 + jnp.arange(1536)
    chip, rest = feature // 48, feature % 48
    spots = jnp.stack([chip // 16, chip // 4 % 4, chip % 4])
    rel = slot_of((spots - me[:, None]) % 4, step[:, None])
    order2 = (rel[2] * 4 + rel[0]) * 4 + rel[1]
    sel_b = low((order2 * 16 + rest // 24 * 8 + 7)[None] == jnp.arange(1024)[:, None])
    key_b = low((rest % 24)[:, None] == jnp.arange(128)[None])
    return sel_b, key_b


def shards(
    tokens, store_keys, store_values, retrieved, seq_lengths,
    w_query, w_key, w_value, w_out, c_query, c_out, ffn_in, ffn_bias, ffn_out,
    gain_self, shift_self, gain_cross, shift_cross, gain_ffn, shift_ffn, cotangent,
):
    core = lax.axis_index("c")
    first = core == 0
    me = jnp.stack([lax.axis_index(a) for a in CHIP])

    def columns(w, which=core):
        n = w.shape[1] // 2
        return lax.dynamic_slice_in_dim(w, which * n, n, 1)

    def rows(w):
        n = w.shape[0] // 2
        return lax.dynamic_slice_in_dim(w, core * n, n, 0)

    def in_order(mine, other, dim):
        return jnp.where(
            first, jnp.concatenate([mine, other], dim), jnp.concatenate([other, mine], dim)
        )

    kv_mine = jnp.concatenate([columns(store_keys), columns(store_values)], 1)
    kv_other = swap(jnp.concatenate([columns(store_keys, 1 - core), columns(store_values, 1 - core)], 1))
    kv = lax.all_gather(in_order(kv_mine, kv_other, 0), CHIP, axis=0, tiled=True)

    tok = both(tokens)
    lengths = both(seq_lengths)
    cot = both(cotangent)
    bias_own = make_mask(retrieved)
    bias_other = swap(bias_own)

    wq, wk, wv, wo = columns(w_query), columns(w_key), columns(w_value), rows(w_out)
    cq, co = columns(c_query), rows(c_out)
    fi, fo = columns(ffn_in), rows(ffn_out)
    fb = lax.dynamic_slice_in_dim(ffn_bias, core * 1536, 1536, 0)[None]
    at, slot, step = slot_tables(me, core)
    table = jnp.concatenate([at.reshape(12), slot.reshape(12)]).astype(jnp.int32)
    natural, turned, sel_v, key_v = place_matrices(me, step)
    sel_b, key_b = bias_matrices(me, step, core)
    core_at = core.reshape(1)
    norms = [a[None] for a in (gain_self, shift_self, gain_cross, shift_cross, gain_ffn, shift_ffn)]

    q, k, v, o_full, o, part = self_fwd(tok, wq, wk, wv, wo, lengths)
    h1, n1, r1, low1, c = self_out(part, swap(part), tok, norms[0], norms[1], cq)
    o_theirs = swap(o)
    (c, fi, fo, fb, cot, norms, natural, turned, sel_v, key_v, sel_b, key_b, o_theirs) = lax.optimization_barrier(
        (c, fi, fo, fb, cot, norms, natural, turned, sel_v, key_v, sel_b, key_b, o_theirs)
    )
    x_full, lse, part = cross_fwd(kv.reshape(64, 128, 768), bias_own, bias_other, c, co)
    x = low(x_full)
    h2, n2, r2, low2, g, gp, part = ffn_fwd(part, swap(part), h1, norms[2], norms[3], fi, fb, fo)
    out, e3, f, dg_ffn, ds_ffn, du, db, part = ffn_bwd(
        part, swap(part), h2, cot, norms[4], norms[5], fi, fo, gp
    )
    e2, y, dg_cross, ds_cross, dx = cross_in(part, swap(part), e3, n2, r2, norms[2], co)

    early = early_grads(core_at, low2, du, x, swap(x), y, g, swap(g), f, natural)
    early = lax.psum_scatter(early.reshape(8192, 384), "x", scatter_dimension=0, tiled=True)

    kv6 = kv.reshape(4, 4, 4, 128, 768)
    own6 = bias_own.reshape(4, 4, 4, 128, 128)
    other6 = bias_other.reshape(4, 4, 4, 128, 128)
    dcs, got, store = [None] * 3, [None] * 3, [None] * 3

    def half_bwd(p, init, *earlier):
        return cross_bwd(table, kv6, own6, other6, after(c, *earlier), dx, x_full, lse, p, init)

    send, dc = half_bwd(2, None)
    got[2] = first_swap(send, "z")
    keep, dcs[2] = half_bwd(2, dc)
    send, dc = half_bwd(1, None, dcs[2])
    got[1] = first_swap(send, "y")
    store[2] = second_swap(keep, got[2], "z")
    keep, dcs[1] = half_bwd(1, dc, got[2])
    send, dc = half_bwd(0, None, dcs[1])
    got[0] = first_swap(send, "x")
    store[1] = second_swap(keep, got[1], "y")
    keep, dcs[0] = half_bwd(0, dc, got[1], store[2])
    dc = jnp.concatenate(dcs, 1)
    part = after(nt(dc, cq), early, store[1])
    early = lax.psum_scatter(early, "y", scatter_dimension=0, tiled=True)
    e1, z, dg_self, ds_self, dq, dk, dv, part = self_bwd(
        part, swap(part), e2, n1, r1, norms[0], wo, q, k, v, o_full, lengths, wq, wk, wv
    )
    theirs = swap(part)
    store[0] = second_swap(keep, got[0], "x")
    z = after(z, got[0])
    gains = jnp.concatenate([dg_self, dg_cross, dg_ffn], 0)
    shifts = jnp.concatenate([ds_self, ds_cross, ds_ffn], 0)
    late = late_grads(
        core_at, tok, low1, o, o_theirs, dq, dk, dv, dc, z, gains, shifts, db, *turned, sel_v, key_v, sel_b, key_b
    )
    late = list(late)
    late[0], early, theirs = lax.optimization_barrier((late[0], early, theirs))
    early = lax.psum_scatter(early, "z", scatter_dimension=0, tiled=True)
    d_tok = part[:128] + theirs[128:] + e1
    late_got = [first_swap(late[2 * p + 1], "xyz"[p]) for p in range(3)]
    sums = []
    for p in range(3):
        late_sum = second_swap(late[2 * p], late_got[p], "xyz"[p])
        sums.append(next_axis([store[p], late_sum], ORDERS[p][1]))
    sums = [next_axis([sums[p]], ORDERS[p][2]) for p in range(3)]
    mine = jnp.concatenate([total([sums[p]], 0) for p in range(3)], 0)
    e_mine = early.astype(F32)
    (
        d_keys, d_values, d_wq, d_cq, d_wk, d_wo, d_wv, d_co, d_fi, d_fo, d_fb, g0, s0, g1, s1, g2, s2
    ) = finish(core_at, mine, swap(mine), e_mine, swap(e_mine))
    return (
        out, d_tok, d_keys, d_values, d_wq, d_wk, d_wv, d_wo, d_cq, d_co, d_fi, d_fb[0], d_fo,
        g0[0], s0[0], g1[0], s1[0], g2[0], s2[0],
    )


def solution(mesh):
    grid = Mesh(mesh.devices.reshape(4, 4, 4, 2), ALL)
    split, line, whole = P(ALL, None), P(ALL), P()
    return jax.shard_map(
        shards,
        mesh=grid,
        in_specs=(split,) * 4 + (line,) + (whole,) * 15 + (split,),
        out_specs=(split,) * 11 + (line,) + (split,) + (line,) * 6,
        check_vma=False,
    )
```

```python
import functools
import math

import jax
import jax.numpy as jnp
from jax import lax
from jax.experimental import pallas as pl
from jax.experimental.pallas import tpu as pltpu
from jax.sharding import Mesh, PartitionSpec as P

F32 = jnp.float32
BF = jnp.bfloat16
LOWEST = -1e30
LOG2E = math.log2(math.e)
SCALE = 64 ** (-0.5)
CHIP = ("x", "y", "z")
ALL = ("x", "y", "z", "c")
ORDERS = (("x", "y", "z"), ("y", "z", "x"), ("z", "x", "y"))


def low(v):
    return v.astype(BF)


def nn(a, b):
    return jnp.dot(a, b, preferred_element_type=F32)


def nt(a, b):
    return lax.dot_general(a, b, (((1,), (1,)), ((), ())), preferred_element_type=F32)


def tn(a, b):
    return lax.dot_general(a, b, (((0,), (0,)), ((), ())), preferred_element_type=F32)


def mask_body(ret_ref, out_ref, m_ref):
    hi_io = lax.broadcasted_iota(jnp.int32, (64, 1024), 0)
    lo_io = lax.broadcasted_iota(jnp.int32, (128, 1024), 0)

    def group(g, carry):
        idx = ret_ref[pl.ds(pl.multiple_of(g * 8, 8), 8), :]
        hi, lo = idx >> 7, idx & 127
        for j in range(8):
            hot_hi = jnp.where(hi_io == hi[j : j + 1, :], 1.0, 0.0).astype(BF)
            hot_lo = jnp.where(lo_io == lo[j : j + 1, :], 1.0, 0.0).astype(BF)
            m_ref[g * 8 + j] = nt(hot_hi, hot_lo)
        return carry

    lax.fori_loop(0, 16, group, 0)

    def flip(h, carry):
        out_ref[h] = ((m_ref[:, h, :].T - 1.0) * 1e30).astype(BF)
        return carry

    lax.fori_loop(0, 64, flip, 0)


VM = pl.BlockSpec(memory_space=pltpu.VMEM)
SM = pl.BlockSpec(memory_space=pltpu.SMEM)
def room(mib):
    return pltpu.CompilerParams(vmem_limit_bytes=mib * 2**20)


def cost(us):
    return pl.CostEstimate(flops=int(us * 1e9), bytes_accessed=int(us * 3e6), transcendentals=0)


def shaped(shape, dtype=F32):
    return jax.ShapeDtypeStruct(shape, dtype)


def make_mask(retrieved):
    return pl.pallas_call(
        mask_body,
        out_shape=shaped((64, 128, 128), BF),
        in_specs=[VM],
        out_specs=VM,
        scratch_shapes=[pltpu.VMEM((128, 64, 128), F32)],
        compiler_params=room(16),
        name="mask",
        cost_estimate=cost(25),
    )(retrieved)


def one_head(a, h, dim):
    at = lax.broadcasted_iota(jnp.int32, a.shape, dim)
    keep = (at < 64) if h == 0 else (at >= 64)
    return jnp.where(keep, a, jnp.zeros_like(a))


def fwd_body(kv_hbm, b0_ref, b1_ref, c_ref, co_ref, kv, x_ref, l_ref, part_ref, acc, ms, ls, cts, buf0, buf1, sem):
    copies = [
        pltpu.make_async_copy(kv_hbm.at[pl.ds(16 * i, 16)], kv.at[pl.ds(16 * i, 16)], sem.at[i]) for i in range(4)
    ]
    for copy in copies:
        copy.start()

    def rows(ref, first, chips, lanes):
        return ref[pl.ds(first, chips), :, lanes].reshape(chips * 128, 128)

    def bias(first, chips):
        every = slice(0, 128)
        return jnp.concatenate([rows(b0_ref, first, chips, every), rows(b1_ref, first, chips, every)], 1).astype(F32)

    def lanes_of(p, shift):
        return pl.ds(pl.multiple_of(shift + p * 128, 128), 128)

    def scores(kk, p, h, extra):
        return nn(kk, cts[p, h]) * (LOG2E * SCALE) + extra

    def weigh(vt, h, probs):
        ones = jnp.ones((16, vt.shape[1]), BF)
        return nn(jnp.concatenate([vt[h * 64 : (h + 1) * 64], ones], 0), probs)

    for p in range(3):
        ct = c_ref[:, p * 128 : (p + 1) * 128].astype(F32).T.astype(BF)
        for h in range(2):
            cts[p, h] = one_head(ct, h, 0)
    copies[0].wait()
    for p in range(3):
        kk = rows(kv, 0, 8, slice(p * 128, (p + 1) * 128))
        for h in range(2):
            ms[p, h] = jnp.max(scores(kk, p, h, bias(0, 8)), 0, keepdims=True)
    acc[...] = jnp.zeros_like(acc)
    ls[...] = jnp.zeros_like(ls)

    def first(n, buf):
        i, p = n // 3, n % 3
        kk, extra = rows(kv, i * 8, 8, lanes_of(p, 0)), bias(i * 8, 8)
        t = [scores(kk, p, h, extra) - ms[p, h] for h in range(2)]
        for h in range(2):
            buf[h] = jnp.exp2(t[h]).astype(BF)

    def second(n, buf):
        i, p = n // 3, n % 3
        vt = rows(kv, i * 8, 8, lanes_of(p, 384)).T
        got = [weigh(vt, h, buf[h]) for h in range(2)]
        for h in range(2):
            acc[p, h] += got[h][0:64]
            ls[p, h] += got[h][64:65]

    first(0, buf0)

    def fast(k, carry):
        for j in range(1, 4):

            @pl.when(k == 3 * j - 1)
            def _(j=j):
                copies[j].wait()

        first(2 * k + 1, buf1)
        second(2 * k, buf0)
        first(jnp.minimum(2 * k + 2, 23), buf0)
        second(2 * k + 1, buf1)
        return carry

    lax.fori_loop(0, 12, fast, 0)
    good = jnp.where((ls[...] < 1e30) & (ls[...] > 1e-30) & (ms[...] > -1e29), 1.0, 0.0)

    @pl.when(jnp.min(good) < 0.5)
    def _():
        acc[...] = jnp.zeros_like(acc)
        ls[...] = jnp.zeros_like(ls)
        ms[...] = jnp.full_like(ms, LOWEST)

        def slow(i, carry):
            def pair(p, carry):
                kk = rows(kv, i * 4, 4, lanes_of(p, 0))
                vt = rows(kv, i * 4, 4, lanes_of(p, 384)).T
                for h in range(2):
                    t = scores(kk, p, h, bias(i * 4, 4))
                    top = jnp.maximum(ms[p, h], jnp.max(t, 0, keepdims=True))
                    shrink = jnp.exp2(ms[p, h] - top)
                    got = weigh(vt, h, jnp.exp2(t - top).astype(BF))
                    acc[p, h] = acc[p, h] * shrink + got[0:64]
                    ls[p, h] = ls[p, h] * shrink + got[64:65]
                    ms[p, h] = top
                return carry

            return lax.fori_loop(0, 3, pair, carry)

        lax.fori_loop(0, 16, slow, 0)

    for p in range(3):
        xs = []
        for h in range(2):
            xs.append(acc[p, h] / ls[p, h])
            l_ref[p, h] = ms[p, h] + jnp.log2(ls[p, h])
        x_ref[:, p * 128 : (p + 1) * 128] = jnp.concatenate(xs, 0).T
    part_ref[...] = nn(x_ref[...].astype(BF), co_ref[...])


def cross_fwd(kv, b0, b1, c, co):
    return pl.pallas_call(
        fwd_body,
        in_specs=[pl.BlockSpec(memory_space=pltpu.HBM)] + [VM] * 4,
        out_specs=[VM] * 4,
        out_shape=[shaped((64, 128, 768), BF), shaped((256, 384)), shaped((3, 2, 1, 256)), shaped((256, 768))],
        scratch_shapes=[
            pltpu.VMEM((3, 2, 64, 256), F32), pltpu.VMEM((3, 2, 1, 256), F32), pltpu.VMEM((3, 2, 1, 256), F32),
            pltpu.VMEM((3, 2, 128, 256), BF), pltpu.VMEM((2, 1024, 256), BF), pltpu.VMEM((2, 1024, 256), BF),
            pltpu.SemaphoreType.DMA((4,)),
        ],
        compiler_params=room(20),
        name="cross_fwd",
        cost_estimate=cost(20),
    )(kv, b0, b1, c, co)


def bwd_body(tab_ref, kv_ref, b0_ref, b1_ref, c_ref, dx_ref, x_ref, l_ref, cq_ref, before_ref, send, keep, dc_ref, part_ref, acc, *, part):
    acc[...] = jnp.zeros_like(acc)
    mid, far = (part + 1) % 3, (part + 2) % 3
    lanes = slice(part * 128, (part + 1) * 128)
    c, dx = c_ref[:, lanes], dx_ref[:, lanes]
    ct = c.astype(F32).T.astype(BF)
    dxt = dx.astype(F32).T
    prod = dxt * x_ref[:, lanes].T * SCALE
    dxt = (dxt * SCALE).astype(BF)
    delta = [jnp.sum(prod[h * 64 : (h + 1) * 64], 0, keepdims=True) for h in range(2)]
    cth = [one_head(ct, h, 0) for h in range(2)]
    dxth = [one_head(dxt, h, 0) for h in range(2)]
    ch = [one_head(c, h, 1) for h in range(2)]
    dxh = [one_head(dx, h, 1) for h in range(2)]

    def slots(first, out):
        def step(g, carry):
            a0 = tab_ref[part * 4 + g + first]

            def pick(ref, j, lanes):
                blocks = []
                for i in (2 * j, 2 * j + 1):
                    blk = ref[a0, i, :, :, lanes] if part == 0 else ref[:, a0, i, :, lanes] if part == 1 else ref[i, :, a0, :, lanes]
                    blocks.append(blk.reshape(512, 128))
                return jnp.concatenate(blocks, 0)

            every = slice(0, 128)
            for j in range(2):
                kk, vv = pick(kv_ref, j, lanes), pick(kv_ref, j, slice(384 + part * 128, 512 + part * 128))
                kt = kk.T
                bias = jnp.concatenate([pick(b0_ref, j, every), pick(b1_ref, j, every)], 1).astype(F32)
                dk, dv = 0.0, 0.0
                for h in range(2):
                    p = jnp.exp2(nn(kk, cth[h]) * (LOG2E * SCALE) + bias - l_ref[part, h])
                    ds = (p * (nn(vv, dxth[h]) - delta[h])).astype(BF)
                    dv = dv + nn(p.astype(BF), dxh[h])
                    dk = dk + nn(ds, ch[h])
                    acc[h * 64 : (h + 1) * 64] += nn(kt[h * 64 : (h + 1) * 64], ds)
                dk = dk.astype(BF).reshape(2, 4, 128, 128)
                dv = dv.astype(BF).reshape(2, 4, 128, 128)
                for i in range(2):
                    for k in range(4):
                        at = tab_ref[12 + mid * 4 + 2 * j + i] * 4 + tab_ref[12 + far * 4 + k]
                        out[g, at, 0:128] = dk[i, k]
                        out[g, at, 128:256] = dv[i, k]
            return carry

        lax.fori_loop(0, 2, step, 0)

    slots(2, send)
    slots(0, keep)
    dc = acc[...].T.astype(BF)
    dc_ref[...] = dc
    part_ref[...] = before_ref[...] + nt(dc, cq_ref[:, lanes])


def cross_bwd(tab, kv, b0, b1, c, dx, x, lse, cq, before, part):
    return pl.pallas_call(
        functools.partial(bwd_body, part=part),
        in_specs=[SM] + [VM] * 9,
        out_specs=[VM] * 4,
        out_shape=[shaped((2, 16, 256, 128), BF)] * 2 + [shaped((256, 128), BF), shaped((256, 768))],
        scratch_shapes=[pltpu.VMEM((128, 256), F32)],
        compiler_params=room(14),
        name="cross_bwd",
        cost_estimate=cost(15),
    )(tab, kv, b0, b1, c, dx, x, lse, cq, before)


def norm_parts(summed, gain, shift):
    average = jnp.mean(summed, -1, keepdims=True)
    centred = summed - average
    spread = lax.rsqrt(jnp.mean(centred * centred, -1, keepdims=True) + 1e-05)
    normed = centred * spread
    return normed * gain + shift, normed, spread


def norm_grad(upstream, normed, spread, gain):
    scaled = upstream * gain
    grad = spread * (
        scaled
        - jnp.mean(scaled, -1, keepdims=True)
        - normed * jnp.mean(scaled * normed, -1, keepdims=True)
    )
    return grad, jnp.sum(upstream * normed, 0, keepdims=True), jnp.sum(upstream, 0, keepdims=True)


def crossed(mine_ref, theirs_ref):
    return jnp.concatenate(
        [mine_ref[0:128] + theirs_ref[128:256], mine_ref[128:256] + theirs_ref[0:128]], 0
    )


def ffn_fwd_body(mine, theirs, h1, norms, fi, fb, fo, h2_ref, n2_ref, r2_ref, low2_ref, g_ref, gp_ref, part_ref):
    h2, n2, r2 = norm_parts(h1[...] + crossed(mine, theirs), norms[2:3], norms[3:4])
    h2_ref[...] = h2
    n2_ref[...] = n2
    r2_ref[...] = r2
    low2_ref[...] = h2.astype(BF)
    total = 0.0
    for j in range(4):
        lanes = slice(j * 384, (j + 1) * 384)
        u = nn(low2_ref[...], fi[:, lanes]) + fb[:, lanes]
        cdf = 0.5 * (1.0 + lax.erf(u * (2.0**-0.5)))
        g = (u * cdf).astype(BF)
        g_ref[:, lanes] = g
        gp_ref[:, lanes] = cdf + u * (jnp.exp(-0.5 * u * u) * ((2.0 * math.pi) ** -0.5))
        total = total + nn(g, fo[lanes, :])
    part_ref[...] = total


def ffn_fwd(*args):
    return pl.pallas_call(
        ffn_fwd_body,
        in_specs=[VM] * 7,
        out_specs=[VM] * 7,
        out_shape=[
            shaped((256, 768)), shaped((256, 768)), shaped((256, 1)), shaped((256, 768), BF),
            shaped((256, 1536), BF), shaped((256, 1536)), shaped((256, 768)),
        ],
        compiler_params=room(16),
        name="ffn_fwd",
        cost_estimate=cost(6),
    )(*args)


def ffn_bwd_body(mine, theirs, h2, cot, norms, fi, fo, gp, out_ref, e3_ref, f_ref, dg_ref, ds_ref, du_ref, db_ref, part_ref):
    out, n3, r3 = norm_parts(h2[...] + crossed(mine, theirs), norms[4:5], norms[5:6])
    out_ref[...] = out[0:128]
    e3, dg_ref[...], ds_ref[...] = norm_grad(cot[...], n3, r3, norms[4:5])
    e3_ref[...] = e3
    f_ref[...] = e3.astype(BF)
    total = 0.0
    for j in range(4):
        lanes = slice(j * 384, (j + 1) * 384)
        du = (nt(f_ref[...], fo[lanes, :]) * gp[:, lanes]).astype(BF)
        du_ref[:, lanes] = du
        db_ref[:, lanes] = jnp.sum(du.astype(F32), 0, keepdims=True)
        total = total + nt(du, fi[:, lanes])
    part_ref[...] = total


def ffn_bwd(*args):
    return pl.pallas_call(
        ffn_bwd_body,
        in_specs=[VM] * 8,
        out_specs=[VM] * 8,
        out_shape=[
            shaped((128, 768)), shaped((256, 768)), shaped((256, 768), BF), shaped((1, 768)), shaped((1, 768)),
            shaped((256, 1536), BF), shaped((1, 1536)), shaped((256, 768)),
        ],
        compiler_params=room(16),
        name="ffn_bwd",
        cost_estimate=cost(6),
    )(*args)


def cross_in_body(mine, theirs, e3, n2, r2, norms, co, e2_ref, y_ref, dg_ref, ds_ref, dx_ref):
    e2, dg_ref[...], ds_ref[...] = norm_grad(e3[...] + crossed(mine, theirs), n2[...], r2[...], norms[2:3])
    e2_ref[...] = e2
    y = e2.astype(BF)
    y_ref[...] = y
    dx_ref[...] = nt(y, co[...]).astype(BF)


def cross_in(mine, theirs, e3, n2, r2, gain, co):
    return pl.pallas_call(
        cross_in_body,
        in_specs=[VM] * 7,
        out_specs=[VM] * 5,
        out_shape=[shaped((256, 768)), shaped((256, 768), BF), shaped((1, 768)), shaped((1, 768)), shaped((256, 384), BF)],
        compiler_params=room(12),
        name="cross_in",
        cost_estimate=cost(4),
    )(mine, theirs, e3, n2, r2, gain, co)


def half_of(core_ref, a_ref):
    n = a_ref.shape[1] // 2
    return jnp.where(core_ref[0] == 0, a_ref[:, 0:n], a_ref[:, n:])


def joined_heads(core_ref, mine, theirs):
    other = jnp.concatenate([theirs[128:256], theirs[0:128]], 0)
    left = jnp.where(core_ref[0] == 0, mine, other)
    right = jnp.where(core_ref[0] == 0, other, mine)
    return jnp.concatenate([left, right], 1)


def early_body(core_ref, low2, du, x, x_theirs, y, g, g_theirs, f, pm, out):
    a = nn(low2[...], pm[...]).astype(BF).T
    for j in range(4):
        out[:, j * 16 : (j + 1) * 16, :] = (
            nn(a, du[:, j * 384 : (j + 1) * 384]).astype(BF).reshape(64, 16, 384)
        )
    a = nn(joined_heads(core_ref, x[...], x_theirs), pm[...]).astype(BF).T
    out[:, 64:80, :] = nn(a, half_of(core_ref, y)).astype(BF).reshape(64, 16, 384)
    g_all = joined_heads(core_ref, g[...], g_theirs)
    fh = half_of(core_ref, f)
    for j in range(4):
        block = nn(g_all[:, j * 768 : (j + 1) * 768].T, fh).astype(BF)
        out[j * 16 : (j + 1) * 16, 80:128, :] = block.reshape(16, 48, 384)


def early_grads(*args):
    return pl.pallas_call(
        early_body,
        in_specs=[SM] + [VM] * 9,
        out_specs=VM,
        out_shape=shaped((64, 128, 384), BF),
        compiler_params=room(24),
        name="early_grads",
        cost_estimate=cost(8),
    )(*args)


def self_in_body(mine, theirs, e2, n1, r1, norms, w4, e1_ref, z_ref, dg_ref, ds_ref, do_ref):
    e1, dg_ref[...], ds_ref[...] = norm_grad(e2[...] + crossed(mine, theirs), n1[...], r1[...], norms[0:1])
    e1_ref[...] = e1[0:128]
    z = e1.astype(BF)
    z_ref[...] = z
    do_ref[...] = nn(z, w4[:, 1152:1536]).astype(BF)


def self_bwd_body(mine, theirs, e2, n1, r1, norms, w4, q_ref, k_ref, v_ref, of_ref, len_ref,
                  z_ref, dg_ref, ds_ref, dq_ref, dk_ref, dv_ref, part_ref, send_ref, do_ref, e1_ref):
    self_in_body(mine, theirs, e2, n1, r1, norms, w4, e1_ref, z_ref, dg_ref, ds_ref, do_ref)
    at_q = lax.broadcasted_iota(jnp.int32, (128, 128), 0)
    at_k = lax.broadcasted_iota(jnp.int32, (128, 128), 1)
    for b in range(2):
        rows = slice(b * 128, (b + 1) * 128)
        allowed = (at_k <= at_q) & (at_k < len_ref[b])
        for pair in range(3):
            cols = slice(pair * 128, (pair + 1) * 128)
            q2, k2, v2, do2 = q_ref[rows, cols], k_ref[rows, cols], v_ref[rows, cols], do_ref[rows, cols]
            of2 = of_ref[rows, cols]
            prod = do2.astype(F32) * of2
            dq2, dk2, dv2 = 0.0, 0.0, 0.0
            for h in range(2):
                kh, vh, qh, doh = (one_head(a, h, 1) for a in (k2, v2, q2, do2))
                s = jnp.where(allowed, nt(q2, kh) * SCALE, LOWEST)
                p = jnp.exp(s - jnp.max(s, -1, keepdims=True))
                p = p / jnp.sum(p, -1, keepdims=True)
                eps = jnp.sum(one_head(prod, h, 1), -1, keepdims=True)
                ds = (p * (nt(do2, vh) - eps) * SCALE).astype(BF)
                dq2 = dq2 + nn(ds, kh)
                dk2 = dk2 + tn(ds, qh)
                dv2 = dv2 + tn(p.astype(BF), doh)
            dq_ref[rows, cols] = dq2.astype(BF)
            dk_ref[rows, cols] = dk2.astype(BF)
            dv_ref[rows, cols] = dv2.astype(BF)
    total = sum(nt(ref[...], w4[:, n * 384 : (n + 1) * 384]) for n, ref in enumerate((dq_ref, dk_ref, dv_ref)))
    part_ref[...] = total[0:128] + e1_ref[...]
    send_ref[...] = total[128:256]


def self_bwd(mine, theirs, e2, n1, r1, norms, w4, q, k, v, of, lengths):
    half = shaped((256, 384), BF)
    return pl.pallas_call(
        self_bwd_body,
        in_specs=[VM] * 11 + [SM],
        out_specs=[VM] * 8,
        out_shape=[
            shaped((256, 768), BF), shaped((1, 768)), shaped((1, 768)),
            half, half, half, shaped((128, 768)), shaped((128, 768)),
        ],
        scratch_shapes=[pltpu.VMEM((256, 384), BF), pltpu.VMEM((128, 768), F32)],
        compiler_params=room(16),
        name="self_bwd",
        cost_estimate=cost(8),
    )(mine, theirs, e2, n1, r1, norms, w4, q, k, v, of, lengths)


def self_fwd_body(tok, w4, len_ref, q_ref, k_ref, v_ref, of_ref, o_ref, part_ref):
    t = tok[...]
    for n, ref in enumerate((q_ref, k_ref, v_ref)):
        ref[...] = nn(t, w4[:, n * 384 : (n + 1) * 384]).astype(BF)
    at_q = lax.broadcasted_iota(jnp.int32, (128, 128), 0)
    at_k = lax.broadcasted_iota(jnp.int32, (128, 128), 1)
    for b in range(2):
        rows = slice(b * 128, (b + 1) * 128)
        allowed = (at_k <= at_q) & (at_k < len_ref[b])
        for pair in range(3):
            cols = slice(pair * 128, (pair + 1) * 128)
            q2, k2, v2 = q_ref[rows, cols], k_ref[rows, cols], v_ref[rows, cols]
            o2 = 0.0
            for h in range(2):
                s = jnp.where(allowed, nt(q2, one_head(k2, h, 1)) * SCALE, LOWEST)
                p = jnp.exp(s - jnp.max(s, -1, keepdims=True))
                p = p / jnp.sum(p, -1, keepdims=True)
                o2 = o2 + nn(p.astype(BF), one_head(v2, h, 1))
            of_ref[rows, cols] = o2
            o_ref[rows, cols] = o2.astype(BF)
    part_ref[...] = nt(o_ref[...], w4[:, 1152:1536])


def self_fwd(tok, w4, lengths):
    half = shaped((256, 384), BF)
    return pl.pallas_call(
        self_fwd_body,
        in_specs=[VM] * 2 + [pl.BlockSpec(memory_space=pltpu.SMEM)],
        out_specs=[VM] * 6,
        out_shape=[half, half, half, shaped((256, 384)), half, shaped((256, 768))],
        compiler_params=room(16),
        name="self_fwd",
        cost_estimate=cost(6),
    )(tok, w4, lengths)


def self_out_body(mine, theirs, tok, norms, cq, h1_ref, n1_ref, r1_ref, low1_ref, c_ref):
    h1, n1, r1 = norm_parts(tok[...].astype(F32) + crossed(mine, theirs), norms[0:1], norms[1:2])
    h1_ref[...] = h1
    n1_ref[...] = n1
    r1_ref[...] = r1
    low1 = h1.astype(BF)
    low1_ref[...] = low1
    c_ref[...] = nn(low1, cq[...]).astype(BF)


def self_out(mine, theirs, tok, norms, cq):
    return pl.pallas_call(
        self_out_body,
        in_specs=[VM] * 5,
        out_specs=[VM] * 5,
        out_shape=[
            shaped((256, 768)), shaped((256, 768)), shaped((256, 1)), shaped((256, 768), BF), shaped((256, 384), BF)
        ],
        compiler_params=room(12),
        name="self_out",
        cost_estimate=cost(3),
    )(mine, theirs, tok, norms, cq)


def place_body(core_ref, tok, low1, o, o_theirs, pm0, pm1, pm2, out):
    joined = joined_heads(core_ref, o[...], o_theirs)
    for n, (a, pm) in enumerate(((tok[...], pm0), (low1[...], pm0), (tok[...], pm1), (joined, pm1), (tok[...], pm2))):
        out[n] = nn(a, pm[...]).astype(BF).T


def place_rows(*args):
    return pl.pallas_call(
        place_body,
        in_specs=[SM] + [VM] * 7,
        out_specs=VM,
        out_shape=shaped((5, 1024, 256), BF),
        compiler_params=room(20),
        name="place_rows",
        cost_estimate=cost(6),
    )(*args)


def late_body(core_ref, placed, dq, dk, dv, dc0, dc1, dc2, z, g0, g1, g2, s0, s1, s2, bias, sel_v, key_v, sel_b, key_b, spread, *outs):
    def put(number, slot, a, b):
        full = nn(placed[a], b)
        if number == 2:
            rows = nn(sel_b[...] * bias[...].astype(BF), key_b[...])
            for v, (gain, shift) in enumerate(((g0, s0), (g1, s1), (g2, s2))):
                vec = jnp.where(core_ref[0] == 0, gain[...], shift[...]).astype(BF)
                rows = rows + nn(sel_v[...] * vec, key_v[v])
            full = jnp.concatenate([full[:, 0:128] + nn(spread[...], rows.astype(BF)), full[:, 128:]], 1)
        full = full.astype(BF)
        for lane in range(3):
            piece = full[:, lane * 128 : (lane + 1) * 128].reshape(4, 16, 16, 128)
            at = slice(slot * 48 + lane * 16, slot * 48 + lane * 16 + 16)
            for d in range(4):
                outs[number * 2 + d // 2][d % 2, :, at, :] = piece[d]

    put(0, 0, 0, dq[...])
    put(0, 1, 1, jnp.concatenate([dc0[...], dc1[...], dc2[...]], 1))
    put(1, 0, 2, dk[...])
    put(1, 1, 3, half_of(core_ref, z))
    put(2, 0, 4, dv[...])


def late_grads(*args):
    sizes = (96, 96, 48)
    return pl.pallas_call(
        late_body,
        in_specs=[SM] + [VM] * 20,
        out_specs=[VM] * 6,
        out_shape=[shaped((2, 16, sizes[n // 2], 128), BF) for n in range(6)],
        compiler_params=room(24),
        name="late_grads",
        cost_estimate=cost(6),
    )(*args)


def finish_body(core_ref, mine, theirs, t_mine, t_theirs, d_tok, keys, values, wq, cq, wk, wo, wv, co, fi, fo, fb, g0, s0, g1, s1, g2, s2):
    first = core_ref[0] == 0
    d_tok[...] = t_mine[...] + t_theirs[...]

    def pick(size, half, base):
        a, b = mine[base : base + 2 * size, :], theirs[base : base + 2 * size, :]
        chosen = jnp.where(first, a, b) if half == 0 else jnp.where(first, b, a)
        return jnp.where(first, chosen[0:size], chosen[size:])

    bases = (0, 352, 704)
    for half in range(2):
        for p in range(3):
            lanes = slice(half * 384 + p * 128, half * 384 + (p + 1) * 128)
            keys[:, lanes] = pick(64, half, bases[p])
            values[:, lanes] = pick(64, half, bases[p] + 128)
        for lane in range(3):
            lanes = slice(half * 384 + lane * 128, half * 384 + (lane + 1) * 128)
            for ref, base in ((wq, 256), (cq, 304), (wk, 608), (wo, 656), (wv, 960)):
                ref[:, lanes] = pick(8, half, base + lane * 16)[0:6]
            early = 1008 + lane * 128
            co[:, lanes] = pick(8, half, early + 64)[0:6]
            fo[:, lanes] = pick(24, half, early + 80)
            for j in range(4):
                at = half * 1536 + j * 384 + lane * 128
                fi[:, at : at + 128] = pick(8, half, early + j * 16)[0:6]
    small = [pick(8, half, 960) for half in range(2)]
    for half, refs in enumerate(((g0, g1, g2), (s0, s1, s2))):
        for v, ref in enumerate(refs):
            ref[...] = small[half][6:7, v * 6 : v * 6 + 6]
    fb[...] = small[0][6:7, 24:48] + small[1][6:7, 24:48]


def finish(*args):
    w, row = shaped((6, 768)), shaped((1, 6))
    return pl.pallas_call(
        finish_body,
        in_specs=[pl.BlockSpec(memory_space=pltpu.SMEM)] + [VM] * 4,
        out_specs=[VM] * 18,
        out_shape=[
            shaped((128, 768)), shaped((64, 768)), shaped((64, 768)), w, w, w, w, w, w, shaped((6, 3072)), shaped((24, 768)),
            shaped((1, 24)), row, row, row, row, row, row,
        ],
        compiler_params=room(12),
        name="finish",
        cost_estimate=cost(2),
    )(*args)


def swap(v):
    return lax.ppermute(v, "c", [(0, 1), (1, 0)])


def partner(v, axis, sign):
    pairs = []
    for i in range(4):
        for c in range(2):
            step = sign if (i + c) % 2 == 0 else -sign
            pairs.append((i * 2 + c, (i + step) % 4 * 2 + c))
    return lax.ppermute(v, (axis, "c"), pairs)


def both(v):
    return jnp.concatenate([v, swap(v)], 0)


def after(v, *earlier):
    return lax.optimization_barrier((v, earlier))[0]


def first_swap(send, axis, *earlier):
    return partner(after(send, *earlier), axis, 1)


def second_swap(keep, got, axis, *earlier):
    pass_on = low(keep[1].astype(F32) + got[1].astype(F32))
    return [keep, got, partner(after(pass_on, *earlier), axis, -1)]


def total(groups, rows):
    parts = [
        keep[0, rows].astype(F32) + got[0, rows].astype(F32) + passed[rows].astype(F32) for keep, got, passed in groups
    ]
    return jnp.concatenate(parts, 1) if len(parts) > 1 else parts[0]


def next_axis(groups, axis):
    n = groups[0][2].shape[0] // 2
    send, keep = low(total(groups, slice(n, 2 * n))), low(total(groups, slice(0, n)))
    send, keep = (a.reshape((2, n // 2) + a.shape[1:]) for a in (send, keep))
    return second_swap(keep, first_swap(send, axis), axis)


def slot_tables(me, core):
    step = jnp.where((me + core) % 2 == 0, 1, -1)
    at = jnp.stack([me, me - step, me + step, me + 2], 1) % 4
    away = (jnp.arange(4)[None] - me[:, None]) % 4
    slot = slot_of(away, step[:, None])
    return at, slot, step


def slot_of(away, step):
    near = jnp.where((away == 1) == (step > 0), 2, 1)
    return jnp.where(away == 0, 0, jnp.where(away == 2, 3, near))


def place_matrices(me, step):
    feature = jnp.arange(768)
    chip, rest = feature // 12, feature % 12
    slot = rest // 6 * 8 + rest % 6
    spots = jnp.stack([chip // 16, chip // 4 % 4, chip % 4])
    rel = slot_of((spots - me[:, None]) % 4, step[:, None])
    columns = jnp.arange(1024)
    natural = low((chip * 16 + slot)[:, None] == columns[None])
    turned = []
    for p in range(3):
        order = (rel[p] * 4 + rel[(p + 1) % 3]) * 4 + rel[(p + 2) % 3]
        turned.append(low((order * 16 + slot)[:, None] == columns[None]))
    order2 = (rel[2] * 4 + rel[0]) * 4 + rel[1]
    small = jnp.arange(128)
    sel_v = low((order2 * 2 + rest // 6)[None] == small[:, None])
    key_v = low(jnp.stack([(feature % 6 + 6 * v)[:, None] == small[None] for v in range(3)]))
    slots = columns[:, None]
    spread = low((slots // 8 == small[None]) & (slots % 8 == 6))
    return natural, turned, sel_v, key_v, spread


def bias_matrices(me, step, core):
    feature = core * 1536 + jnp.arange(1536)
    chip, rest = feature // 48, feature % 48
    spots = jnp.stack([chip // 16, chip // 4 % 4, chip % 4])
    rel = slot_of((spots - me[:, None]) % 4, step[:, None])
    order2 = (rel[2] * 4 + rel[0]) * 4 + rel[1]
    small = jnp.arange(128)
    sel_b = low((order2 * 2 + rest // 24)[None] == small[:, None])
    key_b = low((rest % 24 + 24)[:, None] == small[None])
    return sel_b, key_b


def shards(
    tokens, store_keys, store_values, retrieved, seq_lengths,
    w_query, w_key, w_value, w_out, c_query, c_out, ffn_in, ffn_bias, ffn_out,
    gain_self, shift_self, gain_cross, shift_cross, gain_ffn, shift_ffn, cotangent,
):
    core = lax.axis_index("c")
    first = core == 0
    me = jnp.stack([lax.axis_index(a) for a in CHIP])

    def columns(w, which=core):
        n = w.shape[1] // 2
        return lax.dynamic_slice_in_dim(w, which * n, n, 1)

    def rows(w):
        n = w.shape[0] // 2
        return lax.dynamic_slice_in_dim(w, core * n, n, 0)

    def in_order(mine, other, dim):
        return jnp.where(
            first, jnp.concatenate([mine, other], dim), jnp.concatenate([other, mine], dim)
        )

    kv_mine = jnp.concatenate([columns(store_keys), columns(store_values)], 1)
    kv_other = swap(jnp.concatenate([columns(store_keys, 1 - core), columns(store_values, 1 - core)], 1))
    kv = lax.all_gather(in_order(kv_mine, kv_other, 0), CHIP, axis=0, tiled=True)

    tok = both(tokens)
    lengths = both(seq_lengths)
    cot = both(cotangent)
    bias_own = make_mask(retrieved)
    bias_other = swap(bias_own)

    w4 = jnp.concatenate([columns(w_query), columns(w_key), columns(w_value), rows(w_out).T], 1)
    cq, co = columns(c_query), rows(c_out)
    fi, fo = columns(ffn_in), rows(ffn_out)
    fb = lax.dynamic_slice_in_dim(ffn_bias, core * 1536, 1536, 0)[None]
    at, slot, step = slot_tables(me, core)
    table = jnp.concatenate([at.reshape(12), slot.reshape(12)]).astype(jnp.int32)
    natural, turned, sel_v, key_v, spread = place_matrices(me, step)
    sel_b, key_b = bias_matrices(me, step, core)
    core_at = core.reshape(1)
    norms = jnp.concatenate([gain_self, shift_self, gain_cross, shift_cross, gain_ffn, shift_ffn]).reshape(6, 768)

    q, k, v, o_full, o, part = self_fwd(tok, w4, lengths)
    h1, n1, r1, low1, c = self_out(part, swap(part), tok, norms, cq)
    placed = place_rows(core_at, tok, low1, o, swap(o), *turned)
    (c, fi, fo, fb, cot, norms, natural, placed, sel_v, key_v, sel_b, key_b, spread) = lax.optimization_barrier(
        (c, fi, fo, fb, cot, norms, natural, placed, sel_v, key_v, sel_b, key_b, spread)
    )
    kv, x_full, lse, part = cross_fwd(kv.reshape(64, 128, 768), bias_own, bias_other, c, co)
    x = low(x_full)
    h2, n2, r2, low2, g, gp, part = ffn_fwd(part, swap(part), h1, norms, fi, fb, fo)
    out, e3, f, dg_ffn, ds_ffn, du, db, part = ffn_bwd(
        part, swap(part), h2, cot, norms, fi, fo, gp
    )
    e2, y, dg_cross, ds_cross, dx = cross_in(part, swap(part), e3, n2, r2, norms, co)

    early = early_grads(core_at, low2, du, x, swap(x), y, g, swap(g), f, natural)
    early = lax.psum_scatter(early.reshape(8192, 384), "x", scatter_dimension=0, tiled=True)

    kv6 = kv.reshape(4, 4, 4, 128, 768)
    own6 = bias_own.reshape(4, 4, 4, 128, 128)
    other6 = bias_other.reshape(4, 4, 4, 128, 128)
    dcs, got, store, keeps = [None] * 3, [None] * 3, [None] * 3, [None] * 3
    part, before = jnp.zeros((256, 768), F32), ()
    for p in (2, 1, 0):
        send, keeps[p], dcs[p], part = cross_bwd(
            table, kv6, own6, other6, after(c, before), dx, x_full, lse, cq, part, p
        )
        got[p] = first_swap(send, "xyz"[p])
        before = dcs[p]
    store[2] = second_swap(keeps[2], got[2], "z")
    part = after(part, got[2])
    early = after(early, dcs[0])
    early = lax.psum_scatter(early, "y", scatter_dimension=0, tiled=True)
    z, dg_self, ds_self, dq, dk, dv, t_mine, t_send = self_bwd(
        part, swap(part), e2, n1, r1, norms, w4, q, k, v, o_full, lengths
    )
    t_theirs = swap(t_send)
    store[1] = second_swap(keeps[1], got[1], "y")
    z = after(z, got[1])
    late = late_grads(
        core_at, placed, dq, dk, dv, *dcs, z, dg_self, dg_cross, dg_ffn, ds_self, ds_cross, ds_ffn, db,
        sel_v, key_v, sel_b, key_b, spread,
    )
    late = list(late)
    late[0], early, t_theirs = lax.optimization_barrier((late[0], early, t_theirs))
    early = lax.psum_scatter(early, "z", scatter_dimension=0, tiled=True)
    store[0] = second_swap(keeps[0], after(got[0], late[1]), "x")
    store = after(store, late[0])
    late_got = [first_swap(late[2 * p + 1], "xyz"[p]) for p in range(3)]
    sums = []
    for p in (2, 1, 0):
        late_sum = second_swap(late[2 * p], late_got[p], "xyz"[p])
        sums.insert(0, [store[p], late_sum])
    sums, early = lax.optimization_barrier((sums, early))
    sums = [next_axis(sums[p], ORDERS[p][1]) for p in range(3)]
    sums = [next_axis([sums[p]], ORDERS[p][2]) for p in range(3)]
    early = early.astype(F32)
    mine = jnp.concatenate(
        [total([sums[p]], 0) for p in range(3)] + [early[:, n * 128 : (n + 1) * 128] for n in range(3)], 0
    )
    (
        d_tok, d_keys, d_values, d_wq, d_cq, d_wk, d_wo, d_wv, d_co, d_fi, d_fo, d_fb, g0, s0, g1, s1, g2, s2
    ) = finish(core_at, mine, swap(mine), t_mine, t_theirs)
    return (
        out, d_tok, d_keys, d_values, d_wq, d_wk, d_wv, d_wo, d_cq, d_co, d_fi, d_fb[0], d_fo,
        g0[0], s0[0], g1[0], s1[0], g2[0], s2[0],
    )


def solution(mesh):
    grid = Mesh(mesh.devices.reshape(4, 4, 4, 2), ALL)
    split, line, whole = P(ALL, None), P(ALL), P()
    return jax.shard_map(
        shards,
        mesh=grid,
        in_specs=(split,) * 4 + (line,) + (whole,) * 15 + (split,),
        out_specs=(split,) * 11 + (line,) + (split,) + (line,) * 6,
        check_vma=False,
    )
```

```python
import functools
import math

import jax
import jax.numpy as jnp
from jax import lax
from jax.experimental import pallas as pl
from jax.experimental.pallas import tpu as pltpu
from jax.sharding import Mesh, PartitionSpec as P

F32 = jnp.float32
BF = jnp.bfloat16
LOWEST = -1e30
LOG2E = math.log2(math.e)
SCALE = 64 ** (-0.5)
CHIP = ("x", "y", "z")
ALL = ("x", "y", "z", "c")
ORDERS = (("x", "y", "z"), ("y", "z", "x"), ("z", "x", "y"))


def low(v):
    return v.astype(BF)


def nn(a, b):
    return jnp.dot(a, b, preferred_element_type=F32)


def nt(a, b):
    return lax.dot_general(a, b, (((1,), (1,)), ((), ())), preferred_element_type=F32)


def tn(a, b):
    return lax.dot_general(a, b, (((0,), (0,)), ((), ())), preferred_element_type=F32)


def mask_body(ret_ref, out_ref, m_ref):
    hi_io = lax.broadcasted_iota(jnp.int32, (64, 1024), 0)
    lo_io = lax.broadcasted_iota(jnp.int32, (128, 1024), 0)

    def group(g, carry):
        idx = ret_ref[pl.ds(pl.multiple_of(g * 8, 8), 8), :]
        hi, lo = idx >> 7, idx & 127
        for j in range(8):
            hot_hi = jnp.where(hi_io == hi[j : j + 1, :], 1.0, 0.0).astype(BF)
            hot_lo = jnp.where(lo_io == lo[j : j + 1, :], 1.0, 0.0).astype(BF)
            m_ref[g * 8 + j] = nt(hot_hi, hot_lo)
        return carry

    lax.fori_loop(0, 16, group, 0)

    def flip(h, carry):
        out_ref[h] = ((m_ref[:, h, :].T - 1.0) * 1e30).astype(BF)
        return carry

    lax.fori_loop(0, 64, flip, 0)


VM = pl.BlockSpec(memory_space=pltpu.VMEM)
SM = pl.BlockSpec(memory_space=pltpu.SMEM)
def room(mib):
    return pltpu.CompilerParams(vmem_limit_bytes=mib * 2**20)


def cost(us):
    return pl.CostEstimate(flops=int(us * 1e9), bytes_accessed=int(us * 3e6), transcendentals=0)


def shaped(shape, dtype=F32):
    return jax.ShapeDtypeStruct(shape, dtype)


def make_mask(retrieved):
    return pl.pallas_call(
        mask_body,
        out_shape=shaped((64, 128, 128), BF),
        in_specs=[VM],
        out_specs=VM,
        scratch_shapes=[pltpu.VMEM((128, 64, 128), F32)],
        compiler_params=room(16),
        name="mask",
        cost_estimate=cost(25),
    )(retrieved)


def one_head(a, h, dim):
    at = lax.broadcasted_iota(jnp.int32, a.shape, dim)
    keep = (at < 64) if h == 0 else (at >= 64)
    return jnp.where(keep, a, jnp.zeros_like(a))


def fwd_body(kv_hbm, b0_ref, b1_ref, c_ref, co_ref, kv, x_ref, l_ref, part_ref, acc, ms, ls, cts, buf0, buf1, sem):
    copies = [
        pltpu.make_async_copy(kv_hbm.at[pl.ds(16 * i, 16)], kv.at[pl.ds(16 * i, 16)], sem.at[i]) for i in range(4)
    ]
    for copy in copies:
        copy.start()

    def rows(ref, first, chips, lanes):
        return ref[pl.ds(first, chips), :, lanes].reshape(chips * 128, 128)

    def bias(first, chips):
        every = slice(0, 128)
        return jnp.concatenate([rows(b0_ref, first, chips, every), rows(b1_ref, first, chips, every)], 1).astype(F32)

    def lanes_of(p, shift):
        return pl.ds(pl.multiple_of(shift + p * 128, 128), 128)

    def scores(kk, p, h, extra):
        return nn(kk, cts[p, h]) * (LOG2E * SCALE) + extra

    def weigh(vt, h, probs):
        ones = jnp.ones((16, vt.shape[1]), BF)
        return nn(jnp.concatenate([vt[h * 64 : (h + 1) * 64], ones], 0), probs)

    for p in range(3):
        ct = c_ref[:, p * 128 : (p + 1) * 128].astype(F32).T.astype(BF)
        for h in range(2):
            cts[p, h] = one_head(ct, h, 0)
    copies[0].wait()
    for p in range(3):
        kk = rows(kv, 0, 8, slice(p * 128, (p + 1) * 128))
        for h in range(2):
            ms[p, h] = jnp.max(scores(kk, p, h, bias(0, 8)), 0, keepdims=True)
    acc[...] = jnp.zeros_like(acc)
    ls[...] = jnp.zeros_like(ls)

    def first(n, buf):
        i, p = n // 3, n % 3
        kk, extra = rows(kv, i * 8, 8, lanes_of(p, 0)), bias(i * 8, 8)
        t = [scores(kk, p, h, extra) - ms[p, h] for h in range(2)]
        for h in range(2):
            buf[h] = jnp.exp2(t[h]).astype(BF)

    def second(n, buf):
        i, p = n // 3, n % 3
        vt = rows(kv, i * 8, 8, lanes_of(p, 384)).T
        got = [weigh(vt, h, buf[h]) for h in range(2)]
        for h in range(2):
            acc[p, h] += got[h][0:64]
            ls[p, h] += got[h][64:65]

    first(0, buf0)

    def fast(k, carry):
        for j in range(1, 4):

            @pl.when(k == 3 * j - 1)
            def _(j=j):
                copies[j].wait()

        first(2 * k + 1, buf1)
        second(2 * k, buf0)
        first(jnp.minimum(2 * k + 2, 23), buf0)
        second(2 * k + 1, buf1)
        return carry

    lax.fori_loop(0, 12, fast, 0)
    good = jnp.where((ls[...] < 1e30) & (ls[...] > 1e-30) & (ms[...] > -1e29), 1.0, 0.0)

    @pl.when(jnp.min(good) < 0.5)
    def _():
        acc[...] = jnp.zeros_like(acc)
        ls[...] = jnp.zeros_like(ls)
        ms[...] = jnp.full_like(ms, LOWEST)

        def slow(i, carry):
            def pair(p, carry):
                kk = rows(kv, i * 4, 4, lanes_of(p, 0))
                vt = rows(kv, i * 4, 4, lanes_of(p, 384)).T
                for h in range(2):
                    t = scores(kk, p, h, bias(i * 4, 4))
                    top = jnp.maximum(ms[p, h], jnp.max(t, 0, keepdims=True))
                    shrink = jnp.exp2(ms[p, h] - top)
                    got = weigh(vt, h, jnp.exp2(t - top).astype(BF))
                    acc[p, h] = acc[p, h] * shrink + got[0:64]
                    ls[p, h] = ls[p, h] * shrink + got[64:65]
                    ms[p, h] = top
                return carry

            return lax.fori_loop(0, 3, pair, carry)

        lax.fori_loop(0, 16, slow, 0)

    for p in range(3):
        xs = []
        for h in range(2):
            xs.append(acc[p, h] / ls[p, h])
            l_ref[p, h] = ms[p, h] + jnp.log2(ls[p, h])
        x_ref[:, p * 128 : (p + 1) * 128] = jnp.concatenate(xs, 0).T
    part_ref[...] = nn(x_ref[...].astype(BF), co_ref[...]).astype(BF)


def cross_fwd(kv, b0, b1, c, co):
    return pl.pallas_call(
        fwd_body,
        in_specs=[pl.BlockSpec(memory_space=pltpu.HBM)] + [VM] * 4,
        out_specs=[VM] * 4,
        out_shape=[shaped((64, 128, 768), BF), shaped((256, 384)), shaped((3, 2, 1, 256)), shaped((256, 768), BF)],
        scratch_shapes=[
            pltpu.VMEM((3, 2, 64, 256), F32), pltpu.VMEM((3, 2, 1, 256), F32), pltpu.VMEM((3, 2, 1, 256), F32),
            pltpu.VMEM((3, 2, 128, 256), BF), pltpu.VMEM((2, 1024, 256), BF), pltpu.VMEM((2, 1024, 256), BF),
            pltpu.SemaphoreType.DMA((4,)),
        ],
        compiler_params=room(20),
        name="cross_fwd",
        cost_estimate=cost(20),
    )(kv, b0, b1, c, co)


def bwd_body(tab_ref, kv_ref, b0_ref, b1_ref, c_ref, dx_ref, x_ref, l_ref, cq_ref, before_ref, send, keep, dc_ref, part_ref, acc, *, part):
    acc[...] = jnp.zeros_like(acc)
    mid, far = (part + 1) % 3, (part + 2) % 3
    lanes = slice(part * 128, (part + 1) * 128)
    c, dx = c_ref[:, lanes], dx_ref[:, lanes]
    ct = c.astype(F32).T.astype(BF)
    dxt = dx.astype(F32).T
    prod = dxt * x_ref[:, lanes].T * SCALE
    dxt = (dxt * SCALE).astype(BF)
    delta = [jnp.sum(prod[h * 64 : (h + 1) * 64], 0, keepdims=True) for h in range(2)]
    cth = [one_head(ct, h, 0) for h in range(2)]
    dxth = [one_head(dxt, h, 0) for h in range(2)]
    ch = [one_head(c, h, 1) for h in range(2)]
    dxh = [one_head(dx, h, 1) for h in range(2)]

    def slots(first, out):
        def step(g, carry):
            a0 = tab_ref[part * 4 + g + first]

            def pick(ref, j, lanes):
                blocks = []
                for i in (2 * j, 2 * j + 1):
                    blk = ref[a0, i, :, :, lanes] if part == 0 else ref[:, a0, i, :, lanes] if part == 1 else ref[i, :, a0, :, lanes]
                    blocks.append(blk.reshape(512, 128))
                return jnp.concatenate(blocks, 0)

            every = slice(0, 128)
            for j in range(2):
                kk, vv = pick(kv_ref, j, lanes), pick(kv_ref, j, slice(384 + part * 128, 512 + part * 128))
                kt = kk.T
                bias = jnp.concatenate([pick(b0_ref, j, every), pick(b1_ref, j, every)], 1).astype(F32)
                dk, dv = 0.0, 0.0
                for h in range(2):
                    p = jnp.exp2(nn(kk, cth[h]) * (LOG2E * SCALE) + bias - l_ref[part, h])
                    ds = (p * (nn(vv, dxth[h]) - delta[h])).astype(BF)
                    dv = dv + nn(p.astype(BF), dxh[h])
                    dk = dk + nn(ds, ch[h])
                    acc[h * 64 : (h + 1) * 64] += nn(kt[h * 64 : (h + 1) * 64], ds)
                dk = dk.astype(BF).reshape(2, 4, 128, 128)
                dv = dv.astype(BF).reshape(2, 4, 128, 128)
                for i in range(2):
                    for k in range(4):
                        at = tab_ref[12 + mid * 4 + 2 * j + i] * 4 + tab_ref[12 + far * 4 + k]
                        out[g, at, 0:128] = dk[i, k]
                        out[g, at, 128:256] = dv[i, k]
            return carry

        lax.fori_loop(0, 2, step, 0)

    slots(2, send)
    slots(0, keep)
    dc = acc[...].T.astype(BF)
    dc_ref[...] = dc
    part_ref[...] = before_ref[...] + nt(dc, cq_ref[:, lanes])


def cross_bwd(tab, kv, b0, b1, c, dx, x, lse, cq, before, part):
    return pl.pallas_call(
        functools.partial(bwd_body, part=part),
        in_specs=[SM] + [VM] * 9,
        out_specs=[VM] * 4,
        out_shape=[shaped((2, 16, 256, 128), BF)] * 2 + [shaped((256, 128), BF), shaped((256, 768))],
        scratch_shapes=[pltpu.VMEM((128, 256), F32)],
        compiler_params=room(14),
        name="cross_bwd",
        cost_estimate=cost(15),
    )(tab, kv, b0, b1, c, dx, x, lse, cq, before)


def norm_parts(summed, gain, shift):
    average = jnp.mean(summed, -1, keepdims=True)
    centred = summed - average
    spread = lax.rsqrt(jnp.mean(centred * centred, -1, keepdims=True) + 1e-05)
    normed = centred * spread
    return normed * gain + shift, normed, spread


def norm_grad(upstream, normed, spread, gain):
    scaled = upstream * gain
    grad = spread * (
        scaled
        - jnp.mean(scaled, -1, keepdims=True)
        - normed * jnp.mean(scaled * normed, -1, keepdims=True)
    )
    return grad, jnp.sum(upstream * normed, 0, keepdims=True), jnp.sum(upstream, 0, keepdims=True)


def crossed(mine_ref, theirs_ref):
    mine, theirs = mine_ref[...].astype(F32), theirs_ref[...].astype(F32)
    return mine + jnp.concatenate([theirs[128:256], theirs[0:128]], 0)


def ffn_fwd_body(mine, theirs, h1, norms, fi, fb, fo, h2_ref, n2_ref, r2_ref, low2_ref, g_ref, gp_ref, part_ref):
    h2, n2, r2 = norm_parts(h1[...] + crossed(mine, theirs), norms[2:3], norms[3:4])
    h2_ref[...] = h2
    n2_ref[...] = n2
    r2_ref[...] = r2
    low2_ref[...] = h2.astype(BF)
    total = 0.0
    for j in range(4):
        lanes = slice(j * 384, (j + 1) * 384)
        u = nn(low2_ref[...], fi[:, lanes]) + fb[:, lanes]
        cdf = 0.5 * (1.0 + lax.erf(u * (2.0**-0.5)))
        g = (u * cdf).astype(BF)
        g_ref[:, lanes] = g
        gp_ref[:, lanes] = cdf + u * (jnp.exp(-0.5 * u * u) * ((2.0 * math.pi) ** -0.5))
        total = total + nn(g, fo[lanes, :])
    part_ref[...] = total.astype(BF)


def ffn_fwd(*args):
    return pl.pallas_call(
        ffn_fwd_body,
        in_specs=[VM] * 7,
        out_specs=[VM] * 7,
        out_shape=[
            shaped((256, 768)), shaped((256, 768)), shaped((256, 1)), shaped((256, 768), BF),
            shaped((256, 1536), BF), shaped((256, 1536)), shaped((256, 768), BF),
        ],
        compiler_params=room(16),
        name="ffn_fwd",
        cost_estimate=cost(6),
    )(*args)


def ffn_bwd_body(mine, theirs, h2, cot, norms, fi, fo, gp, out_ref, e3_ref, f_ref, dg_ref, ds_ref, du_ref, db_ref, part_ref):
    out, n3, r3 = norm_parts(h2[...] + crossed(mine, theirs), norms[4:5], norms[5:6])
    out_ref[...] = out[0:128]
    e3, dg_ref[...], ds_ref[...] = norm_grad(cot[...], n3, r3, norms[4:5])
    e3_ref[...] = e3
    f_ref[...] = e3.astype(BF)
    total = 0.0
    for j in range(4):
        lanes = slice(j * 384, (j + 1) * 384)
        du = (nt(f_ref[...], fo[lanes, :]) * gp[:, lanes]).astype(BF)
        du_ref[:, lanes] = du
        db_ref[:, lanes] = jnp.sum(du.astype(F32), 0, keepdims=True)
        total = total + nt(du, fi[:, lanes])
    part_ref[...] = total.astype(BF)


def ffn_bwd(*args):
    return pl.pallas_call(
        ffn_bwd_body,
        in_specs=[VM] * 8,
        out_specs=[VM] * 8,
        out_shape=[
            shaped((128, 768)), shaped((256, 768)), shaped((256, 768), BF), shaped((1, 768)), shaped((1, 768)),
            shaped((256, 1536), BF), shaped((1, 1536)), shaped((256, 768), BF),
        ],
        compiler_params=room(16),
        name="ffn_bwd",
        cost_estimate=cost(6),
    )(*args)


def cross_in_body(mine, theirs, e3, n2, r2, norms, co, e2_ref, y_ref, dg_ref, ds_ref, dx_ref):
    e2, dg_ref[...], ds_ref[...] = norm_grad(e3[...] + crossed(mine, theirs), n2[...], r2[...], norms[2:3])
    e2_ref[...] = e2
    y = e2.astype(BF)
    y_ref[...] = y
    dx_ref[...] = nt(y, co[...]).astype(BF)


def cross_in(mine, theirs, e3, n2, r2, gain, co):
    return pl.pallas_call(
        cross_in_body,
        in_specs=[VM] * 7,
        out_specs=[VM] * 5,
        out_shape=[shaped((256, 768)), shaped((256, 768), BF), shaped((1, 768)), shaped((1, 768)), shaped((256, 384), BF)],
        compiler_params=room(12),
        name="cross_in",
        cost_estimate=cost(4),
    )(mine, theirs, e3, n2, r2, gain, co)


def half_of(core_ref, a_ref):
    n = a_ref.shape[1] // 2
    return jnp.where(core_ref[0] == 0, a_ref[:, 0:n], a_ref[:, n:])


def joined_heads(core_ref, mine, theirs):
    other = jnp.concatenate([theirs[128:256], theirs[0:128]], 0)
    left = jnp.where(core_ref[0] == 0, mine, other)
    right = jnp.where(core_ref[0] == 0, other, mine)
    return jnp.concatenate([left, right], 1)


def early_body(core_ref, low2, du, x, x_theirs, y, g, g_theirs, f, pm, out):
    a = nn(low2[...], pm[...]).astype(BF).T
    for j in range(4):
        out[:, j * 16 : (j + 1) * 16, :] = (
            nn(a, du[:, j * 384 : (j + 1) * 384]).astype(BF).reshape(64, 16, 384)
        )
    a = nn(joined_heads(core_ref, x[...], x_theirs), pm[...]).astype(BF).T
    out[:, 64:80, :] = nn(a, half_of(core_ref, y)).astype(BF).reshape(64, 16, 384)
    g_all = joined_heads(core_ref, g[...], g_theirs)
    fh = half_of(core_ref, f)
    for j in range(4):
        block = nn(g_all[:, j * 768 : (j + 1) * 768].T, fh).astype(BF)
        out[j * 16 : (j + 1) * 16, 80:128, :] = block.reshape(16, 48, 384)


def early_grads(*args):
    return pl.pallas_call(
        early_body,
        in_specs=[SM] + [VM] * 9,
        out_specs=VM,
        out_shape=shaped((64, 128, 384), BF),
        compiler_params=room(24),
        name="early_grads",
        cost_estimate=cost(8),
    )(*args)


def self_in_body(mine, theirs, e2, n1, r1, norms, w4, e1_ref, z_ref, dg_ref, ds_ref, do_ref):
    e1, dg_ref[...], ds_ref[...] = norm_grad(e2[...] + crossed(mine, theirs), n1[...], r1[...], norms[0:1])
    e1_ref[...] = e1[0:128]
    z = e1.astype(BF)
    z_ref[...] = z
    do_ref[...] = nn(z, w4[:, 1152:1536]).astype(BF)


def self_bwd_body(mine, theirs, e2, n1, r1, norms, w4, q_ref, k_ref, v_ref, of_ref, len_ref,
                  z_ref, dg_ref, ds_ref, dq_ref, dk_ref, dv_ref, part_ref, send_ref, do_ref, e1_ref):
    self_in_body(mine, theirs, e2, n1, r1, norms, w4, e1_ref, z_ref, dg_ref, ds_ref, do_ref)
    at_q = lax.broadcasted_iota(jnp.int32, (128, 128), 0)
    at_k = lax.broadcasted_iota(jnp.int32, (128, 128), 1)
    for b in range(2):
        rows = slice(b * 128, (b + 1) * 128)
        allowed = (at_k <= at_q) & (at_k < len_ref[b])
        for pair in range(3):
            cols = slice(pair * 128, (pair + 1) * 128)
            q2, k2, v2, do2 = q_ref[rows, cols], k_ref[rows, cols], v_ref[rows, cols], do_ref[rows, cols]
            of2 = of_ref[rows, cols]
            prod = do2.astype(F32) * of2
            dq2, dk2, dv2 = 0.0, 0.0, 0.0
            for h in range(2):
                kh, vh, qh, doh = (one_head(a, h, 1) for a in (k2, v2, q2, do2))
                s = jnp.where(allowed, nt(q2, kh) * SCALE, LOWEST)
                p = jnp.exp(s - jnp.max(s, -1, keepdims=True))
                p = p / jnp.sum(p, -1, keepdims=True)
                eps = jnp.sum(one_head(prod, h, 1), -1, keepdims=True)
                ds = (p * (nt(do2, vh) - eps) * SCALE).astype(BF)
                dq2 = dq2 + nn(ds, kh)
                dk2 = dk2 + tn(ds, qh)
                dv2 = dv2 + tn(p.astype(BF), doh)
            dq_ref[rows, cols] = dq2.astype(BF)
            dk_ref[rows, cols] = dk2.astype(BF)
            dv_ref[rows, cols] = dv2.astype(BF)
    total = sum(nt(ref[...], w4[:, n * 384 : (n + 1) * 384]) for n, ref in enumerate((dq_ref, dk_ref, dv_ref)))
    part_ref[...] = total[0:128] + e1_ref[...]
    send_ref[...] = total[128:256]


def self_bwd(mine, theirs, e2, n1, r1, norms, w4, q, k, v, of, lengths):
    half = shaped((256, 384), BF)
    return pl.pallas_call(
        self_bwd_body,
        in_specs=[VM] * 11 + [SM],
        out_specs=[VM] * 8,
        out_shape=[
            shaped((256, 768), BF), shaped((1, 768)), shaped((1, 768)),
            half, half, half, shaped((128, 768)), shaped((128, 768)),
        ],
        scratch_shapes=[pltpu.VMEM((256, 384), BF), pltpu.VMEM((128, 768), F32)],
        compiler_params=room(16),
        name="self_bwd",
        cost_estimate=cost(8),
    )(mine, theirs, e2, n1, r1, norms, w4, q, k, v, of, lengths)


def self_fwd_body(tok, w4, len_ref, q_ref, k_ref, v_ref, of_ref, o_ref, part_ref):
    t = tok[...]
    for n, ref in enumerate((q_ref, k_ref, v_ref)):
        ref[...] = nn(t, w4[:, n * 384 : (n + 1) * 384]).astype(BF)
    at_q = lax.broadcasted_iota(jnp.int32, (128, 128), 0)
    at_k = lax.broadcasted_iota(jnp.int32, (128, 128), 1)
    for b in range(2):
        rows = slice(b * 128, (b + 1) * 128)
        allowed = (at_k <= at_q) & (at_k < len_ref[b])
        for pair in range(3):
            cols = slice(pair * 128, (pair + 1) * 128)
            q2, k2, v2 = q_ref[rows, cols], k_ref[rows, cols], v_ref[rows, cols]
            o2 = 0.0
            for h in range(2):
                s = jnp.where(allowed, nt(q2, one_head(k2, h, 1)) * SCALE, LOWEST)
                p = jnp.exp(s - jnp.max(s, -1, keepdims=True))
                p = p / jnp.sum(p, -1, keepdims=True)
                o2 = o2 + nn(p.astype(BF), one_head(v2, h, 1))
            of_ref[rows, cols] = o2
            o_ref[rows, cols] = o2.astype(BF)
    part_ref[...] = nt(o_ref[...], w4[:, 1152:1536]).astype(BF)


def self_fwd(tok, w4, lengths):
    half = shaped((256, 384), BF)
    return pl.pallas_call(
        self_fwd_body,
        in_specs=[VM] * 2 + [pl.BlockSpec(memory_space=pltpu.SMEM)],
        out_specs=[VM] * 6,
        out_shape=[half, half, half, shaped((256, 384)), half, shaped((256, 768), BF)],
        compiler_params=room(16),
        name="self_fwd",
        cost_estimate=cost(6),
    )(tok, w4, lengths)


def self_out_body(mine, theirs, tok, norms, cq, h1_ref, n1_ref, r1_ref, low1_ref, c_ref):
    h1, n1, r1 = norm_parts(tok[...].astype(F32) + crossed(mine, theirs), norms[0:1], norms[1:2])
    h1_ref[...] = h1
    n1_ref[...] = n1
    r1_ref[...] = r1
    low1 = h1.astype(BF)
    low1_ref[...] = low1
    c_ref[...] = nn(low1, cq[...]).astype(BF)


def self_out(mine, theirs, tok, norms, cq):
    return pl.pallas_call(
        self_out_body,
        in_specs=[VM] * 5,
        out_specs=[VM] * 5,
        out_shape=[
            shaped((256, 768)), shaped((256, 768)), shaped((256, 1)), shaped((256, 768), BF), shaped((256, 384), BF)
        ],
        compiler_params=room(12),
        name="self_out",
        cost_estimate=cost(3),
    )(mine, theirs, tok, norms, cq)


def place_body(core_ref, tok, low1, o, o_theirs, pm0, pm1, pm2, out):
    joined = joined_heads(core_ref, o[...], o_theirs)
    for n, (a, pm) in enumerate(((tok[...], pm0), (low1[...], pm0), (tok[...], pm1), (joined, pm1), (tok[...], pm2))):
        out[n] = nn(a, pm[...]).astype(BF).T


def place_rows(*args):
    return pl.pallas_call(
        place_body,
        in_specs=[SM] + [VM] * 7,
        out_specs=VM,
        out_shape=shaped((5, 1024, 256), BF),
        compiler_params=room(20),
        name="place_rows",
        cost_estimate=cost(6),
    )(*args)


def late_body(core_ref, placed, dq, dk, dv, dc0, dc1, dc2, z, g0, g1, g2, s0, s1, s2, bias, sel_v, key_v, sel_b, key_b, spread, *outs):
    def put(number, slot, a, b):
        full = nn(placed[a], b)
        if number == 2:
            rows = nn(sel_b[...] * bias[...].astype(BF), key_b[...])
            for v, (gain, shift) in enumerate(((g0, s0), (g1, s1), (g2, s2))):
                vec = jnp.where(core_ref[0] == 0, gain[...], shift[...]).astype(BF)
                rows = rows + nn(sel_v[...] * vec, key_v[v])
            full = jnp.concatenate([full[:, 0:128] + nn(spread[...], rows.astype(BF)), full[:, 128:]], 1)
        full = full.astype(BF)
        for lane in range(3):
            piece = full[:, lane * 128 : (lane + 1) * 128].reshape(4, 16, 16, 128)
            at = slice(slot * 48 + lane * 16, slot * 48 + lane * 16 + 16)
            for d in range(4):
                outs[number * 2 + d // 2][d % 2, :, at, :] = piece[d]

    put(0, 0, 0, dq[...])
    put(0, 1, 1, jnp.concatenate([dc0[...], dc1[...], dc2[...]], 1))
    put(1, 0, 2, dk[...])
    put(1, 1, 3, half_of(core_ref, z))
    put(2, 0, 4, dv[...])


def late_grads(*args):
    sizes = (96, 96, 48)
    return pl.pallas_call(
        late_body,
        in_specs=[SM] + [VM] * 20,
        out_specs=[VM] * 6,
        out_shape=[shaped((2, 16, sizes[n // 2], 128), BF) for n in range(6)],
        compiler_params=room(24),
        name="late_grads",
        cost_estimate=cost(6),
    )(*args)


def finish_body(core_ref, mine, theirs, t_mine, t_theirs, d_tok, keys, values, wq, cq, wk, wo, wv, co, fi, fo, fb, g0, s0, g1, s1, g2, s2):
    first = core_ref[0] == 0
    d_tok[...] = t_mine[...] + t_theirs[...]

    def pick(size, half, base):
        a, b = mine[base : base + 2 * size, :], theirs[base : base + 2 * size, :]
        chosen = jnp.where(first, a, b) if half == 0 else jnp.where(first, b, a)
        return jnp.where(first, chosen[0:size], chosen[size:])

    bases = (0, 352, 704)
    for half in range(2):
        for p in range(3):
            lanes = slice(half * 384 + p * 128, half * 384 + (p + 1) * 128)
            keys[:, lanes] = pick(64, half, bases[p])
            values[:, lanes] = pick(64, half, bases[p] + 128)
        for lane in range(3):
            lanes = slice(half * 384 + lane * 128, half * 384 + (lane + 1) * 128)
            for ref, base in ((wq, 256), (cq, 304), (wk, 608), (wo, 656), (wv, 960)):
                ref[:, lanes] = pick(8, half, base + lane * 16)[0:6]
            early = 1008 + lane * 128
            co[:, lanes] = pick(8, half, early + 64)[0:6]
            fo[:, lanes] = pick(24, half, early + 80)
            for j in range(4):
                at = half * 1536 + j * 384 + lane * 128
                fi[:, at : at + 128] = pick(8, half, early + j * 16)[0:6]
    small = [pick(8, half, 960) for half in range(2)]
    for half, refs in enumerate(((g0, g1, g2), (s0, s1, s2))):
        for v, ref in enumerate(refs):
            ref[...] = small[half][6:7, v * 6 : v * 6 + 6]
    fb[...] = small[0][6:7, 24:48] + small[1][6:7, 24:48]


def finish(*args):
    w, row = shaped((6, 768)), shaped((1, 6))
    return pl.pallas_call(
        finish_body,
        in_specs=[pl.BlockSpec(memory_space=pltpu.SMEM)] + [VM] * 4,
        out_specs=[VM] * 18,
        out_shape=[
            shaped((128, 768)), shaped((64, 768)), shaped((64, 768)), w, w, w, w, w, w, shaped((6, 3072)), shaped((24, 768)),
            shaped((1, 24)), row, row, row, row, row, row,
        ],
        compiler_params=room(12),
        name="finish",
        cost_estimate=cost(2),
    )(*args)


def swap(v):
    return lax.ppermute(v, "c", [(0, 1), (1, 0)])


def partner(v, axis, sign):
    pairs = []
    for i in range(4):
        for c in range(2):
            step = sign if (i + c) % 2 == 0 else -sign
            pairs.append((i * 2 + c, (i + step) % 4 * 2 + c))
    return lax.ppermute(v, (axis, "c"), pairs)


def both(v):
    return jnp.concatenate([v, swap(v)], 0)


def after(v, *earlier):
    return lax.optimization_barrier((v, earlier))[0]


def first_swap(send, axis, *earlier):
    return partner(after(send, *earlier), axis, 1)


def second_swap(keep, got, axis, *earlier):
    pass_on = low(keep[1].astype(F32) + got[1].astype(F32))
    return [keep, got, partner(after(pass_on, *earlier), axis, -1)]


def total(groups, rows):
    parts = [
        keep[0, rows].astype(F32) + got[0, rows].astype(F32) + passed[rows].astype(F32) for keep, got, passed in groups
    ]
    return jnp.concatenate(parts, 1) if len(parts) > 1 else parts[0]


def next_axis(groups, axis):
    n = groups[0][2].shape[0] // 2
    send, keep = low(total(groups, slice(n, 2 * n))), low(total(groups, slice(0, n)))
    send, keep = (a.reshape((2, n // 2) + a.shape[1:]) for a in (send, keep))
    return second_swap(keep, first_swap(send, axis), axis)


def slot_tables(me, core):
    step = jnp.where((me + core) % 2 == 0, 1, -1)
    at = jnp.stack([me, me - step, me + step, me + 2], 1) % 4
    away = (jnp.arange(4)[None] - me[:, None]) % 4
    slot = slot_of(away, step[:, None])
    return at, slot, step


def slot_of(away, step):
    near = jnp.where((away == 1) == (step > 0), 2, 1)
    return jnp.where(away == 0, 0, jnp.where(away == 2, 3, near))


def place_matrices(me, step):
    feature = jnp.arange(768)
    chip, rest = feature // 12, feature % 12
    slot = rest // 6 * 8 + rest % 6
    spots = jnp.stack([chip // 16, chip // 4 % 4, chip % 4])
    rel = slot_of((spots - me[:, None]) % 4, step[:, None])
    columns = jnp.arange(1024)
    natural = low((chip * 16 + slot)[:, None] == columns[None])
    turned = []
    for p in range(3):
        order = (rel[p] * 4 + rel[(p + 1) % 3]) * 4 + rel[(p + 2) % 3]
        turned.append(low((order * 16 + slot)[:, None] == columns[None]))
    order2 = (rel[2] * 4 + rel[0]) * 4 + rel[1]
    small = jnp.arange(128)
    sel_v = low((order2 * 2 + rest // 6)[None] == small[:, None])
    key_v = low(jnp.stack([(feature % 6 + 6 * v)[:, None] == small[None] for v in range(3)]))
    slots = columns[:, None]
    spread = low((slots // 8 == small[None]) & (slots % 8 == 6))
    return natural, turned, sel_v, key_v, spread


def bias_matrices(me, step, core):
    feature = core * 1536 + jnp.arange(1536)
    chip, rest = feature // 48, feature % 48
    spots = jnp.stack([chip // 16, chip // 4 % 4, chip % 4])
    rel = slot_of((spots - me[:, None]) % 4, step[:, None])
    order2 = (rel[2] * 4 + rel[0]) * 4 + rel[1]
    small = jnp.arange(128)
    sel_b = low((order2 * 2 + rest // 24)[None] == small[:, None])
    key_b = low((rest % 24 + 24)[:, None] == small[None])
    return sel_b, key_b


def shards(
    tokens, store_keys, store_values, retrieved, seq_lengths,
    w_query, w_key, w_value, w_out, c_query, c_out, ffn_in, ffn_bias, ffn_out,
    gain_self, shift_self, gain_cross, shift_cross, gain_ffn, shift_ffn, cotangent,
):
    core = lax.axis_index("c")
    first = core == 0
    me = jnp.stack([lax.axis_index(a) for a in CHIP])

    def columns(w, which=core):
        n = w.shape[1] // 2
        return lax.dynamic_slice_in_dim(w, which * n, n, 1)

    def rows(w):
        n = w.shape[0] // 2
        return lax.dynamic_slice_in_dim(w, core * n, n, 0)

    def in_order(mine, other, dim):
        return jnp.where(
            first, jnp.concatenate([mine, other], dim), jnp.concatenate([other, mine], dim)
        )

    kv_mine = jnp.concatenate([columns(store_keys), columns(store_values)], 1)
    kv_other = swap(jnp.concatenate([columns(store_keys, 1 - core), columns(store_values, 1 - core)], 1))
    kv = lax.all_gather(in_order(kv_mine, kv_other, 0), CHIP, axis=0, tiled=True)

    tok = both(tokens)
    lengths = both(seq_lengths)
    cot = both(cotangent)
    bias_own = make_mask(retrieved)
    bias_other = swap(bias_own)

    w4 = jnp.concatenate([columns(w_query), columns(w_key), columns(w_value), rows(w_out).T], 1)
    cq, co = columns(c_query), rows(c_out)
    fi, fo = columns(ffn_in), rows(ffn_out)
    fb = lax.dynamic_slice_in_dim(ffn_bias, core * 1536, 1536, 0)[None]
    at, slot, step = slot_tables(me, core)
    table = jnp.concatenate([at.reshape(12), slot.reshape(12)]).astype(jnp.int32)
    natural, turned, sel_v, key_v, spread = place_matrices(me, step)
    sel_b, key_b = bias_matrices(me, step, core)
    core_at = core.reshape(1)
    norms = jnp.concatenate([gain_self, shift_self, gain_cross, shift_cross, gain_ffn, shift_ffn]).reshape(6, 768)

    q, k, v, o_full, o, part = self_fwd(tok, w4, lengths)
    h1, n1, r1, low1, c = self_out(part, swap(part), tok, norms, cq)
    placed = place_rows(core_at, tok, low1, o, swap(o), *turned)
    (c, fi, fo, fb, cot, norms, natural, placed, sel_v, key_v, sel_b, key_b, spread) = lax.optimization_barrier(
        (c, fi, fo, fb, cot, norms, natural, placed, sel_v, key_v, sel_b, key_b, spread)
    )
    kv, x_full, lse, part = cross_fwd(kv.reshape(64, 128, 768), bias_own, bias_other, c, co)
    x = low(x_full)
    h2, n2, r2, low2, g, gp, part = ffn_fwd(part, swap(part), h1, norms, fi, fb, fo)
    out, e3, f, dg_ffn, ds_ffn, du, db, part = ffn_bwd(
        part, swap(part), h2, cot, norms, fi, fo, gp
    )
    e2, y, dg_cross, ds_cross, dx = cross_in(part, swap(part), e3, n2, r2, norms, co)

    early = early_grads(core_at, low2, du, x, swap(x), y, g, swap(g), f, natural)
    early = lax.psum_scatter(early.reshape(8192, 384), "x", scatter_dimension=0, tiled=True)

    kv6 = kv.reshape(4, 4, 4, 128, 768)
    own6 = bias_own.reshape(4, 4, 4, 128, 128)
    other6 = bias_other.reshape(4, 4, 4, 128, 128)
    dcs, got, store, keeps = [None] * 3, [None] * 3, [None] * 3, [None] * 3
    part, before = jnp.zeros((256, 768), F32), ()
    for p in (2, 1, 0):
        send, keeps[p], dcs[p], part = cross_bwd(
            table, kv6, own6, other6, after(c, before), dx, x_full, lse, cq, part, p
        )
        got[p] = first_swap(send, "xyz"[p])
        before = dcs[p]
    store[2] = second_swap(keeps[2], got[2], "z")
    part = after(part, got[2])
    early = after(early, dcs[0])
    early = lax.psum_scatter(early, "y", scatter_dimension=0, tiled=True)
    z, dg_self, ds_self, dq, dk, dv, t_mine, t_send = self_bwd(
        part, swap(part), e2, n1, r1, norms, w4, q, k, v, o_full, lengths
    )
    t_theirs = swap(t_send)
    store[1] = second_swap(keeps[1], got[1], "y")
    z = after(z, got[1])
    late = late_grads(
        core_at, placed, dq, dk, dv, *dcs, z, dg_self, dg_cross, dg_ffn, ds_self, ds_cross, ds_ffn, db,
        sel_v, key_v, sel_b, key_b, spread,
    )
    late = list(late)
    late[0], early, t_theirs = lax.optimization_barrier((late[0], early, t_theirs))
    early = lax.psum_scatter(early, "z", scatter_dimension=0, tiled=True)
    store[0] = second_swap(keeps[0], after(got[0], late[1]), "x")
    store = after(store, late[0])
    late_got = [first_swap(late[2 * p + 1], "xyz"[p]) for p in range(3)]
    sums = []
    for p in (2, 1, 0):
        late_sum = second_swap(late[2 * p], late_got[p], "xyz"[p])
        sums.insert(0, [store[p], late_sum])
    sums, early = lax.optimization_barrier((sums, early))
    sums = [next_axis(sums[p], ORDERS[p][1]) for p in range(3)]
    sums = [next_axis([sums[p]], ORDERS[p][2]) for p in range(3)]
    early = early.astype(F32)
    mine = jnp.concatenate(
        [total([sums[p]], 0) for p in range(3)] + [early[:, n * 128 : (n + 1) * 128] for n in range(3)], 0
    )
    (
        d_tok, d_keys, d_values, d_wq, d_cq, d_wk, d_wo, d_wv, d_co, d_fi, d_fo, d_fb, g0, s0, g1, s1, g2, s2
    ) = finish(core_at, mine, swap(mine), t_mine, t_theirs)
    return (
        out, d_tok, d_keys, d_values, d_wq, d_wk, d_wv, d_wo, d_cq, d_co, d_fi, d_fb[0], d_fo,
        g0[0], s0[0], g1[0], s1[0], g2[0], s2[0],
    )


def solution(mesh):
    grid = Mesh(mesh.devices.reshape(4, 4, 4, 2), ALL)
    split, line, whole = P(ALL, None), P(ALL), P()
    return jax.shard_map(
        shards,
        mesh=grid,
        in_specs=(split,) * 4 + (line,) + (whole,) * 15 + (split,),
        out_specs=(split,) * 11 + (line,) + (split,) + (line,) * 6,
        check_vma=False,
    )
```
